256 devices in a mesh: row: 16 (over z, core), col: 16 (over x, y).
Axes of the slice: x: 4, y: 4, z: 8, core: 2. Of those that a mesh axis runs over, the one named last changes fastest.
Arguments:
- diag_tile: float32 [128, 128], P('row'), may hold values from -20 to 100, as said below
- panel: bfloat16 [32768, 128], P(('row', 'col')), may hold values from -1.796875 to 1.796875
- trailing: float32 [32768, 8192], P('row', 'col'), may hold values from -6 to 6
Outputs:
- solved: bfloat16 [32768, 128], P(('row', 'col'))
- updated: float32 [32768, 8192], P('row', 'col')
The draws below stay inside these ranges and needn't reach their ends.
Inputs may be any that keep to these rules, and one draw needn't show every extreme that they name: diag_tile is symmetric and positive definite, with its smallest eigenvalue 1 or more.
All inputs are finite; a program needn't handle non-finite values.
Results may differ from the reference program's by a relative error of at most 0.0051.
Values may be sent and summed in bfloat16 or wider, within the bound.
A program may use at most 64 MiB of HBM per device.

```python
import math
import jax
import jax.numpy as jnp
from jax import lax

PANEL = 128
ROW_DEV = 2048
ROWS = 32768
COLS = 8192
N_ROW = 16


def draw_diag_tile(key, part):
    key_gram = jax.random.fold_in(key, 11)
    key_shift = jax.random.fold_in(key, 12)
    factor_draw = jax.random.normal(key_gram, (PANEL, PANEL), jnp.float32) / math.sqrt(PANEL)
    gram = jnp.dot(factor_draw, factor_draw.T, precision=lax.Precision.HIGHEST)
    gram = 0.5 * (gram + gram.T)
    shifts = jnp.exp(jax.random.uniform(key_shift, (PANEL,), jnp.float32, 0.0, math.log(4.0)))
    matrix_tile = gram + jnp.diag(shifts)
    return matrix_tile


def block_levels(key, dims, split, smallest, top_value):
    loudness = 1.0
    for dim, shards_of in split:
        heights = jax.random.uniform(jax.random.fold_in(jax.random.fold_in(key, 6), dim), (shards_of,), jnp.float32, smallest / len(split), top_value / len(split))
        loudness = loudness * jnp.repeat(jnp.exp(heights), dims[dim] // shards_of).reshape((-1,) + (1,) * (len(dims) - 1 - dim))
    return loudness


def gaussian(stream_key, dims, scale, bound, pieces=(), kind=jnp.bfloat16):
    drawn = jax.random.normal(stream_key, dims, jnp.float32) * scale
    if len(pieces) > 0:
        drawn = block_levels(stream_key, dims, pieces, -0.22, 0.18) * drawn
    return jnp.clip(drawn, min=-bound, max=bound).astype(kind)


def setup_inputs(seed: int = 0) -> dict:
    key_of = jax.random.split(jax.random.key(seed), 4)
    diag_tile = draw_diag_tile(jax.random.fold_in(key_of[3], 71), 0)
    panel = gaussian(key_of[1], (ROWS, PANEL), 0.3, 1.796875, ((0, 256),))
    trailing = gaussian(key_of[2], (ROWS, COLS), 1.0, 6.0, ((0, 16), (1, 16)), jnp.float32)
    return {"diag_tile": diag_tile, "panel": panel, "trailing": trailing}


def reference(diag_tile, panel, trailing):
    factor = jnp.linalg.cholesky(diag_tile)
    identity = jnp.eye(PANEL, dtype=diag_tile.dtype)
    inverse = lax.linalg.triangular_solve(factor, identity, left_side=True, lower=True).astype(jnp.bfloat16)
    solved = lax.dot_general(panel.astype(jnp.float32), inverse.astype(jnp.float32), (((1,), (1,)), ((), ())), preferred_element_type=jnp.float32).astype(jnp.bfloat16)
    top_rows = solved[:COLS]
    col_ids = jnp.arange(COLS, dtype=jnp.int32)

    def one_block(block_index):
        row_start = block_index * ROW_DEV
        block_rows = lax.dynamic_slice_in_dim(solved, row_start, ROW_DEV, 0)
        old_rows = lax.dynamic_slice_in_dim(trailing, row_start, ROW_DEV, 0)
        update = lax.dot_general(block_rows.astype(jnp.float32), top_rows.astype(jnp.float32), (((1,), (1,)), ((), ())), preferred_element_type=jnp.float32)
        row_ids = row_start + jnp.arange(ROW_DEV, dtype=jnp.int32)
        return jnp.where(row_ids[:, None] >= col_ids[None, :], old_rows - update, old_rows)
    blocks = lax.map(one_block, jnp.arange(N_ROW, dtype=jnp.int32))
    return (solved, blocks.reshape(ROWS, COLS))
```

```python
import functools

import jax
import jax.numpy as jnp
from jax import lax
from jax.experimental import pallas as pl
from jax.experimental.pallas import tpu as pltpu
from jax.sharding import PartitionSpec as P

MESH = pl.DeviceIdType.MESH
HIGHEST = lax.Precision.HIGHEST
N = 16
PANEL = 128
BLOCK = 16
CHUNK = 256


def spread(tile, sublane):
    return jnp.broadcast_to(tile[sublane : sublane + 1, :], (8, 128))


def eliminate(rows, k, lane, sub):
    tiles = BLOCK // 8
    first = BLOCK * k
    column = [
        [
            jnp.broadcast_to(rows[t][:, first + j : first + j + 1], (8, 128)) if t >= j // 8 else None
            for t in range(tiles)
        ]
        for j in range(BLOCK)
    ]
    in_block = (lane >= first) & (lane < first + BLOCK)
    packed = [
        jnp.where(in_block, jnp.where(lane - first == sub + 8 * t, 1.0, 0.0), rows[t]) for t in range(tiles)
    ]
    inverse_pivot = [None] * tiles
    for j in range(BLOCK):
        tj, sj = divmod(j, 8)
        r = 1.0 / spread(column[j][tj], sj)
        scaled = {t: column[j][t] * r for t in range(tj, tiles)}
        for m in range(j + 1, BLOCK):
            s = spread(column[j][m // 8], m % 8)
            for t in range(m // 8, tiles):
                column[m][t] = column[m][t] - scaled[t] * s
        row = spread(packed[tj], sj)
        for t in range(tj, tiles):
            if t == tj and sj == 7:
                continue
            factor = jnp.where(sub > sj, scaled[t], 0.0) if t == tj else scaled[t]
            packed[t] = packed[t] - factor * row
        inverse_pivot[tj] = r if inverse_pivot[tj] is None else jnp.where(sub == sj, r, inverse_pivot[tj])
    return packed, inverse_pivot


def invert_factor(tile_ref, inverse_ref, between):
    lane = lax.broadcasted_iota(jnp.int32, (8, 128), 1)
    sub = lax.broadcasted_iota(jnp.int32, (8, 128), 0)
    blocks, tiles = PANEL // BLOCK, BLOCK // 8
    for k in range(blocks):
        between(k)
        first, after = BLOCK * k, BLOCK * (k + 1)
        rows = [tile_ref[first + 8 * t : first + 8 * t + 8, :] for t in range(tiles)]
        packed, inverse_pivot = eliminate(rows, k, lane, sub)
        inverse = [
            jnp.where(lane < after, packed[t] * jnp.sqrt(inverse_pivot[t]), 0.0) for t in range(tiles)
        ]
        inverse_ref[first:after, :] = jnp.concatenate(inverse, axis=0).astype(jnp.bfloat16)
        if k < blocks - 1:
            left = jnp.concatenate(packed, axis=0).T[after:, :]
            right = jnp.concatenate([packed[t] * inverse_pivot[t] for t in range(tiles)], axis=0)
            change = lax.dot_general(
                left, right, (((1,), (0,)), ((), ())), precision=HIGHEST, preferred_element_type=jnp.float32
            )
            rest = tile_ref[after:, :]
            rest_lane = lax.broadcasted_iota(jnp.int32, rest.shape, 1)
            done = (rest_lane >= first) & (rest_lane < after)
            tile_ref[after:, :] = jnp.where(done, 0.0, rest) - change


def gather_kernel(
    diag_ref, panel_ref, trailing_ref,
    row_ref, col_ref, inverse_ref, slab_ref,
    tile_ref, top_ref, sent_ref, slab_sem, own_sems,
    tile_send, tile_recv, row_send, row_recv, top_send, top_recv, col_send, col_recv,
):
    row, col = lax.axis_index("row"), lax.axis_index("col")
    z, core = row // 2, row % 2
    other = 1 - core

    targets = [8 * layer + 4 * core + col // 4 for layer in range(2)]
    slot = col % 4
    from_other = (col // 4) % 2 != core
    source_core = (col // 4) % 2

    barrier = pltpu.get_barrier_semaphore()

    def greet(device):
        pl.semaphore_signal(barrier, inc=1, device_id=device, device_id_type=MESH)

    for i in range(1, N):
        greet((lax.rem(row + i, N), col))
    for i in range(1, N):
        greet((row, lax.rem(col + i, N)))

    @pl.when(from_other)
    def _():
        for j in range(4):
            greet((2 * z + other, 4 * (col % 4) + j))

    own_tile = tile_ref.at[pl.ds(pl.multiple_of(row * 8, 8), 8), :]
    own_rows = row_ref.at[pl.ds(pl.multiple_of(col * PANEL, PANEL), PANEL), :]
    tile_load = pltpu.make_async_copy(diag_ref, sent_ref, own_sems.at[0])
    tile_load.start()
    rows_load = pltpu.make_async_copy(panel_ref, own_rows, own_sems.at[1])
    rows_load.start()
    slab_copy = pltpu.make_async_copy(trailing_ref, slab_ref, slab_sem)
    slab_copy.start()
    tile_load.wait()
    rows_load.wait()
    own_tile[...] = sent_ref[...]

    @pl.when(z < 2)
    def _():
        top_ref[pl.ds(pl.multiple_of(z * PANEL, PANEL), PANEL), :] = own_rows[...]

    pl.semaphore_wait(barrier, 2 * (N - 1) + 2)

    def tile_copy(to, mine):
        here = tile_ref.at[pl.ds(pl.multiple_of(mine * 8, 8), 8), :]
        return pltpu.make_async_remote_copy(
            src_ref=sent_ref, dst_ref=here, send_sem=tile_send.at[to], recv_sem=tile_recv.at[mine],
            device_id=(to, col), device_id_type=MESH,
        )

    def row_copy(to, mine):
        there = row_ref.at[pl.ds(pl.multiple_of(mine * PANEL, PANEL), PANEL), :]
        return pltpu.make_async_remote_copy(
            src_ref=own_rows, dst_ref=there, send_sem=row_send.at[to], recv_sem=row_recv.at[mine],
            device_id=(row, to), device_id_type=MESH,
        )

    def top_copy(to, layer):
        there = top_ref.at[pl.ds(pl.multiple_of(layer * PANEL, PANEL), PANEL), :]
        return pltpu.make_async_remote_copy(
            src_ref=own_rows, dst_ref=there, send_sem=top_send.at[to], recv_sem=top_recv.at[layer],
            device_id=(2 * to + core, col), device_id_type=MESH,
        )

    def col_copy(layer, to_core, to_slot):
        there = col_ref.at[pl.ds(pl.multiple_of(to_slot * PANEL, PANEL), PANEL), :]
        return pltpu.make_async_remote_copy(
            src_ref=top_ref.at[pl.ds(layer * PANEL, PANEL), :], dst_ref=there,
            send_sem=col_send.at[layer, to_core], recv_sem=col_recv.at[to_slot],
            device_id=(2 * z + to_core, targets[layer]), device_id_type=MESH,
        )

    def is_self(layer):
        return targets[layer] == col

    for i in range(1, N):
        tile_copy(lax.rem(row + i, N), row).start()

    @pl.when(z < 2)
    def _():
        for i in range(1, N // 2):
            top_copy(lax.rem(z + i, N // 2), z).start()

    for i in range(1, N):
        row_copy(lax.rem(col + i, N), col).start()

    for i in range(1, N):
        tile_copy(row, lax.rem(row + i, N)).wait_recv()

    def between(k):
        if k != 4:
            return
        for layer in range(2):

            @pl.when(z != layer)
            def _():
                top_copy(z, layer).wait_recv()

        for layer in range(2):
            col_copy(layer, other, slot).start()

            @pl.when(jnp.logical_not(is_self(layer)))
            def _():
                col_copy(layer, core, slot).start()

            @pl.when(is_self(layer))
            def _():
                col_ref[pl.ds(pl.multiple_of(slot * PANEL, PANEL), PANEL), :] = top_ref[
                    layer * PANEL : (layer + 1) * PANEL, :
                ]

    invert_factor(tile_ref, inverse_ref, between)

    for i in range(1, N):
        row_copy(col, lax.rem(col + i, N)).wait_recv()

    for j in range(4):
        sender = 4 * (col % 4) + j

        @pl.when(jnp.logical_not((sender == col) & (source_core == core)))
        def _():
            col_copy(0, core, j).wait_recv()

    slab_copy.wait()
    for i in range(1, N):
        tile_copy(lax.rem(row + i, N), row).wait_send()

    @pl.when(z < 2)
    def _():
        for i in range(1, N // 2):
            top_copy(lax.rem(z + i, N // 2), z).wait_send()

    for i in range(1, N):
        row_copy(lax.rem(col + i, N), col).wait_send()
    for layer in range(2):
        col_copy(layer, other, slot).wait_send()

        @pl.when(jnp.logical_not(is_self(layer)))
        def _():
            col_copy(layer, core, slot).wait_send()


def update_kernel(row_ref, col_ref, inverse_ref, slab_ref, solved_ref, updated_ref, out_ref, sems):
    row, col = lax.axis_index("row"), lax.axis_index("col")
    rows, cols = slab_ref.shape

    def solve(block):
        return lax.dot_general(
            block, inverse_ref[...], (((1,), (1,)), ((), ())), preferred_element_type=jnp.float32
        ).astype(jnp.bfloat16)

    solved_ref[...] = solve(row_ref[pl.ds(pl.multiple_of(col * PANEL, PANEL), PANEL), :])
    solved_cols = solve(col_ref[...])
    offset = row * rows - col * cols
    below = lax.broadcasted_iota(jnp.int32, (CHUNK, cols), 0) - lax.broadcasted_iota(jnp.int32, (CHUNK, cols), 1)
    copies = []
    for i in range(rows // CHUNK):
        part = pl.ds(i * CHUNK, CHUNK)
        solved_rows = solve(row_ref[part, :])
        change = lax.dot_general(
            solved_rows, solved_cols, (((1,), (1,)), ((), ())), preferred_element_type=jnp.float32
        )
        lower = below >= -(offset + i * CHUNK)
        old = slab_ref[part, :]
        out_ref[part, :] = jnp.where(lower, old - change, old)
        copy = pltpu.make_async_copy(out_ref.at[part, :], updated_ref.at[part, :], sems.at[i])
        copy.start()
        copies.append(copy)
    for copy in copies:
        copy.wait()


def per_device(diag_tile, panel, trailing):
    rows, cols = trailing.shape
    vmem = pl.BlockSpec(memory_space=pltpu.VMEM)
    hbm = pl.BlockSpec(memory_space=pltpu.HBM)
    dma = pltpu.SemaphoreType.DMA
    gathered = pl.pallas_call(
        gather_kernel,
        out_shape=(
            pltpu.VMEM((rows, PANEL), jnp.bfloat16),
            pltpu.VMEM((cols, PANEL), jnp.bfloat16),
            pltpu.VMEM((PANEL, PANEL), jnp.bfloat16),
            pltpu.VMEM((rows, cols), jnp.float32),
        ),
        in_specs=[hbm] * 3,
        out_specs=[vmem] * 4,
        scratch_shapes=[
            pltpu.VMEM((PANEL, PANEL), jnp.float32),
            pltpu.VMEM((2 * PANEL, PANEL), jnp.bfloat16),
            pltpu.VMEM((8, PANEL), jnp.float32),
            dma(()), dma((2,)),
            dma((N,)), dma((N,)), dma((N,)), dma((N,)),
            dma((N // 2,)), dma((2,)), dma((2, 2)), dma((4,)),
        ],
        compiler_params=pltpu.CompilerParams(
            collective_id=0, has_side_effects=True, vmem_limit_bytes=16 << 20
        ),
        name="gather_and_factor",
    )(*[pltpu.with_memory_space_constraint(x, pltpu.HBM) for x in (diag_tile, panel, trailing)])
    return pl.pallas_call(
        update_kernel,
        out_shape=(
            jax.ShapeDtypeStruct((PANEL, PANEL), jnp.bfloat16),
            jax.ShapeDtypeStruct((rows, cols), jnp.float32),
        ),
        in_specs=[vmem] * 4,
        out_specs=[vmem, hbm],
        scratch_shapes=[pltpu.VMEM((rows, cols), jnp.float32), dma((rows // CHUNK,))],
        compiler_params=pltpu.CompilerParams(vmem_limit_bytes=24 << 20),
        name="solve_and_update",
    )(*[pltpu.with_memory_space_constraint(x, pltpu.VMEM) for x in gathered])


def solution(mesh):
    in_specs = (P("row", None), P(("row", "col"), None), P("row", "col"))
    out_specs = (P(("row", "col"), None), P("row", "col"))
    return jax.shard_map(
        per_device, mesh=mesh, in_specs=in_specs, out_specs=out_specs, check_vma=False
    )
```

```python
import functools

import jax
import jax.numpy as jnp
from jax import lax
from jax.experimental import pallas as pl
from jax.experimental.pallas import tpu as pltpu
from jax.sharding import PartitionSpec as P

MESH = pl.DeviceIdType.MESH
HIGHEST = lax.Precision.HIGHEST
N = 16
PANEL = 128
BLOCK = 32
CHUNK = 256


def spread(tile, sublane):
    return jnp.broadcast_to(tile[sublane : sublane + 1, :], (8, 128))


def eliminate(rows, k, lane, sub):
    tiles = BLOCK // 8
    first = BLOCK * k
    column = [
        [
            jnp.broadcast_to(rows[t][:, first + j : first + j + 1], (8, 128)) if t >= j // 8 else None
            for t in range(tiles)
        ]
        for j in range(BLOCK)
    ]
    in_block = (lane >= first) & (lane < first + BLOCK)
    packed = [
        jnp.where(in_block, jnp.where(lane - first == sub + 8 * t, 1.0, 0.0), rows[t]) for t in range(tiles)
    ]
    inverse_pivot = [None] * tiles
    for j in range(BLOCK):
        tj, sj = divmod(j, 8)
        r = 1.0 / spread(column[j][tj], sj)
        scaled = {t: column[j][t] * r for t in range(tj, tiles)}
        for m in range(j + 1, BLOCK):
            s = spread(column[j][m // 8], m % 8)
            for t in range(m // 8, tiles):
                column[m][t] = column[m][t] - scaled[t] * s
        row = spread(packed[tj], sj)
        for t in range(tj, tiles):
            if t == tj and sj == 7:
                continue
            factor = jnp.where(sub > sj, scaled[t], 0.0) if t == tj else scaled[t]
            packed[t] = packed[t] - factor * row
        inverse_pivot[tj] = r if inverse_pivot[tj] is None else jnp.where(sub == sj, r, inverse_pivot[tj])
    return packed, inverse_pivot


def invert_factor(tile_ref, inverse_ref, between):
    lane = lax.broadcasted_iota(jnp.int32, (8, 128), 1)
    sub = lax.broadcasted_iota(jnp.int32, (8, 128), 0)
    blocks, tiles = PANEL // BLOCK, BLOCK // 8
    for k in range(blocks):
        between(k)
        first, after = BLOCK * k, BLOCK * (k + 1)
        rows = [tile_ref[first + 8 * t : first + 8 * t + 8, :] for t in range(tiles)]
        packed, inverse_pivot = eliminate(rows, k, lane, sub)
        inverse = [
            jnp.where(lane < after, packed[t] * jnp.sqrt(inverse_pivot[t]), 0.0) for t in range(tiles)
        ]
        inverse_ref[first:after, :] = jnp.concatenate(inverse, axis=0).astype(jnp.bfloat16)
        if k < blocks - 1:
            left = jnp.concatenate(packed, axis=0).T[after:, :]
            right = jnp.concatenate([packed[t] * inverse_pivot[t] for t in range(tiles)], axis=0)
            change = lax.dot_general(
                left, right, (((1,), (0,)), ((), ())), precision=HIGHEST, preferred_element_type=jnp.float32
            )
            rest = tile_ref[after:, :]
            rest_lane = lax.broadcasted_iota(jnp.int32, rest.shape, 1)
            done = (rest_lane >= first) & (rest_lane < after)
            tile_ref[after:, :] = jnp.where(done, 0.0, rest) - change


def gather_kernel(
    diag_ref, panel_ref, trailing_ref,
    row_ref, col_ref, inverse_ref, slab_ref,
    tile_ref, top_ref, slab_sem,
    tile_send, tile_recv, row_send, row_recv, top_send, top_recv, col_send, col_recv,
    row_ready, plane_ready,
):
    row, col = lax.axis_index("row"), lax.axis_index("col")
    z, core = row // 2, row % 2
    other = 1 - core
    sibling = (2 * z + other, col)

    targets = [8 * layer + 4 * core + col // 4 for layer in range(2)]
    slot = col % 4

    def piece(ref, index, size):
        return ref.at[pl.ds(pl.multiple_of(index * size, size), size), :]

    def wait_for(ref, sem):
        pltpu.make_async_copy(ref, ref, sem).wait()

    barrier = pltpu.get_barrier_semaphore()

    def greet(device):
        pl.semaphore_signal(barrier, inc=1, device_id=device, device_id_type=MESH)

    for i in range(1, N // 2):
        greet((2 * lax.rem(z + i, N // 2), col))
    for i in range(1, N):
        greet((2 * z + 1, lax.rem(col + i, N)))
    greet(sibling)

    pltpu.make_async_copy(diag_ref, piece(tile_ref, row, 8), tile_recv).start()
    pltpu.make_async_copy(panel_ref, piece(row_ref, col, PANEL), row_recv).start()

    @pl.when(z < 2)
    def _():
        pltpu.make_async_copy(panel_ref, piece(top_ref, z, PANEL), top_recv).start()

    def tell(sem):
        pl.semaphore_signal(sem, inc=1, device_id=sibling, device_id_type=MESH)

    @pl.when(core == 0)
    def _():
        pl.semaphore_wait(barrier, N - 1)
        tell(row_ready)

    @pl.when(core == 1)
    def _():
        pl.semaphore_wait(row_ready, 1)

    for i in range(1, N):
        pltpu.make_async_remote_copy(
            src_ref=diag_ref, dst_ref=piece(tile_ref, row, 8), send_sem=tile_send, recv_sem=tile_recv,
            device_id=(lax.rem(row + i, N), col), device_id_type=MESH,
        ).start()

    @pl.when(z < 2)
    def _():
        for i in range(1, N // 2):
            pltpu.make_async_remote_copy(
                src_ref=panel_ref, dst_ref=piece(top_ref, z, PANEL), send_sem=top_send, recv_sem=top_recv,
                device_id=(2 * lax.rem(z + i, N // 2) + core, col), device_id_type=MESH,
            ).start()

    slab_copy = pltpu.make_async_copy(trailing_ref, slab_ref, slab_sem)
    slab_copy.start()

    @pl.when(core == 1)
    def _():
        pl.semaphore_wait(barrier, 2 * N - 1)
        tell(plane_ready)

    @pl.when(core == 0)
    def _():
        pl.semaphore_wait(plane_ready, 1)

    for i in range(1, N):
        pltpu.make_async_remote_copy(
            src_ref=panel_ref, dst_ref=piece(row_ref, col, PANEL), send_sem=row_send, recv_sem=row_recv,
            device_id=(row, lax.rem(col + i, N)), device_id_type=MESH,
        ).start()

    wait_for(tile_ref, tile_recv)

    def between(k):
        if k != 1:
            return
        wait_for(top_ref, top_recv)
        for layer in range(2):
            here, there = top_ref.at[pl.ds(layer * PANEL, PANEL), :], piece(col_ref, slot, PANEL)
            pltpu.make_async_remote_copy(
                src_ref=here, dst_ref=there, send_sem=col_send.at[layer, 0], recv_sem=col_recv,
                device_id=(2 * z + other, targets[layer]), device_id_type=MESH,
            ).start()

            @pl.when(targets[layer] != col)
            def _():
                pltpu.make_async_remote_copy(
                    src_ref=here, dst_ref=there, send_sem=col_send.at[layer, 1], recv_sem=col_recv,
                    device_id=(row, targets[layer]), device_id_type=MESH,
                ).start()

            @pl.when(targets[layer] == col)
            def _():
                pltpu.make_async_copy(here, there, col_recv).start()

    invert_factor(tile_ref, inverse_ref, between)

    wait_for(row_ref, row_recv)
    wait_for(col_ref, col_recv)
    slab_copy.wait()
    wait_for(tile_ref.at[pl.ds(0, (N - 1) * 8), :], tile_send)
    wait_for(row_ref.at[pl.ds(0, (N - 1) * PANEL), :], row_send)

    @pl.when(z < 2)
    def _():
        wait_for(row_ref.at[pl.ds(0, (N // 2 - 1) * PANEL), :], top_send)

    for layer in range(2):
        wait_for(top_ref.at[pl.ds(0, PANEL), :], col_send.at[layer, 0])

        @pl.when(targets[layer] != col)
        def _():
            wait_for(top_ref.at[pl.ds(0, PANEL), :], col_send.at[layer, 1])


def update_kernel(row_ref, col_ref, inverse_ref, slab_ref, solved_ref, updated_ref, out_ref, sems):
    row, col = lax.axis_index("row"), lax.axis_index("col")
    rows, cols = slab_ref.shape

    def solve(block):
        return lax.dot_general(
            block, inverse_ref[...], (((1,), (1,)), ((), ())), preferred_element_type=jnp.float32
        ).astype(jnp.bfloat16)

    solved_ref[...] = solve(row_ref[pl.ds(pl.multiple_of(col * PANEL, PANEL), PANEL), :])
    solved_cols = solve(col_ref[...])
    offset = row * rows - col * cols
    below = lax.broadcasted_iota(jnp.int32, (CHUNK, cols), 0) - lax.broadcasted_iota(jnp.int32, (CHUNK, cols), 1)
    copies = []
    for i in range(rows // CHUNK):
        part = pl.ds(i * CHUNK, CHUNK)
        solved_rows = solve(row_ref[part, :])
        change = lax.dot_general(
            solved_rows, solved_cols, (((1,), (1,)), ((), ())), preferred_element_type=jnp.float32
        )
        lower = below >= -(offset + i * CHUNK)
        old = slab_ref[part, :]
        out_ref[part, :] = jnp.where(lower, old - change, old)
        copy = pltpu.make_async_copy(out_ref.at[part, :], updated_ref.at[part, :], sems.at[i])
        copy.start()
        copies.append(copy)
    for copy in copies:
        copy.wait()


def per_device(diag_tile, panel, trailing):
    rows, cols = trailing.shape
    vmem = pl.BlockSpec(memory_space=pltpu.VMEM)
    hbm = pl.BlockSpec(memory_space=pltpu.HBM)
    dma = pltpu.SemaphoreType.DMA
    gathered = pl.pallas_call(
        gather_kernel,
        out_shape=(
            pltpu.VMEM((rows, PANEL), jnp.bfloat16),
            pltpu.VMEM((cols, PANEL), jnp.bfloat16),
            pltpu.VMEM((PANEL, PANEL), jnp.bfloat16),
            pltpu.VMEM((rows, cols), jnp.float32),
        ),
        in_specs=[hbm] * 3,
        out_specs=[vmem] * 4,
        scratch_shapes=[
            pltpu.VMEM((PANEL, PANEL), jnp.float32),
            pltpu.VMEM((2 * PANEL, PANEL), jnp.bfloat16),
            dma(()),
            dma(()), dma(()), dma(()), dma(()),
            dma(()), dma(()), dma((2, 2)), dma(()),
            pltpu.SemaphoreType.REGULAR, pltpu.SemaphoreType.REGULAR,
        ],
        compiler_params=pltpu.CompilerParams(
            collective_id=0, has_side_effects=True, vmem_limit_bytes=16 << 20
        ),
        name="gather_and_factor",
    )(*[pltpu.with_memory_space_constraint(x, pltpu.HBM) for x in (diag_tile, panel, trailing)])
    return pl.pallas_call(
        update_kernel,
        out_shape=(
            jax.ShapeDtypeStruct((PANEL, PANEL), jnp.bfloat16),
            jax.ShapeDtypeStruct((rows, cols), jnp.float32),
        ),
        in_specs=[vmem] * 4,
        out_specs=[vmem, hbm],
        scratch_shapes=[pltpu.VMEM((rows, cols), jnp.float32), dma((rows // CHUNK,))],
        compiler_params=pltpu.CompilerParams(vmem_limit_bytes=24 << 20),
        name="solve_and_update",
    )(*[pltpu.with_memory_space_constraint(x, pltpu.VMEM) for x in gathered])


def solution(mesh):
    in_specs = (P("row", None), P(("row", "col"), None), P("row", "col"))
    out_specs = (P(("row", "col"), None), P("row", "col"))
    return jax.shard_map(
        per_device, mesh=mesh, in_specs=in_specs, out_specs=out_specs, check_vma=False
    )
```

```python
import functools

import jax
import jax.numpy as jnp
from jax import lax
from jax.experimental import pallas as pl
from jax.experimental.pallas import tpu as pltpu
from jax.sharding import PartitionSpec as P

MESH = pl.DeviceIdType.MESH
HIGHEST = lax.Precision.HIGHEST
N = 16
PANEL = 128
BLOCK = 32
PASS_AT = 2
CHUNK = 256


def spread(tile, sublane):
    return jnp.broadcast_to(tile[sublane : sublane + 1, :], (8, 128))


def eliminate(rows, k, lane, sub):
    tiles = BLOCK // 8
    first = BLOCK * k
    column = [
        [
            jnp.broadcast_to(rows[t][:, first + j : first + j + 1], (8, 128)) if t >= j // 8 else None
            for t in range(tiles)
        ]
        for j in range(BLOCK)
    ]
    in_block = (lane >= first) & (lane < first + BLOCK)
    packed = [
        jnp.where(in_block, jnp.where(lane - first == sub + 8 * t, 1.0, 0.0), rows[t]) for t in range(tiles)
    ]
    inverse_pivot = [None] * tiles
    for j in range(BLOCK):
        tj, sj = divmod(j, 8)
        r = 1.0 / spread(column[j][tj], sj)
        scaled = {t: column[j][t] * r for t in range(tj, tiles)}
        for m in range(j + 1, BLOCK):
            s = spread(column[j][m // 8], m % 8)
            for t in range(m // 8, tiles):
                column[m][t] = column[m][t] - scaled[t] * s
        row = spread(packed[tj], sj)
        for t in range(tj, tiles):
            if t == tj and sj == 7:
                continue
            factor = jnp.where(sub > sj, scaled[t], 0.0) if t == tj else scaled[t]
            packed[t] = packed[t] - factor * row
        inverse_pivot[tj] = r if inverse_pivot[tj] is None else jnp.where(sub == sj, r, inverse_pivot[tj])
    return packed, inverse_pivot


def invert_factor(tile_ref, inverse_ref, between):
    lane = lax.broadcasted_iota(jnp.int32, (8, 128), 1)
    sub = lax.broadcasted_iota(jnp.int32, (8, 128), 0)
    blocks, tiles = PANEL // BLOCK, BLOCK // 8
    for k in range(blocks):
        between(k)
        first, after = BLOCK * k, BLOCK * (k + 1)
        rows = [tile_ref[first + 8 * t : first + 8 * t + 8, :] for t in range(tiles)]
        packed, inverse_pivot = eliminate(rows, k, lane, sub)
        inverse = [
            jnp.where(lane < after, packed[t] * jnp.sqrt(inverse_pivot[t]), 0.0) for t in range(tiles)
        ]
        inverse_ref[first:after, :] = jnp.concatenate(inverse, axis=0).astype(jnp.bfloat16)
        if k < blocks - 1:
            left = jnp.concatenate(packed, axis=0).T[after:, :]
            right = jnp.concatenate([packed[t] * inverse_pivot[t] for t in range(tiles)], axis=0)
            change = lax.dot_general(
                left, right, (((1,), (0,)), ((), ())), precision=HIGHEST, preferred_element_type=jnp.float32
            )
            rest = tile_ref[after:, :]
            rest_lane = lax.broadcasted_iota(jnp.int32, rest.shape, 1)
            done = (rest_lane >= first) & (rest_lane < after)
            tile_ref[after:, :] = jnp.where(done, 0.0, rest) - change


def gather_kernel(
    diag_ref, panel_ref, trailing_ref,
    row_ref, col_ref, inverse_ref, slab_ref,
    tile_ref, slab_sem,
    tile_send, tile_recv, row_send, row_recv, top_recv, half_send, half_recv, pass_send,
    row_ready, plane_ready,
):
    row, col = lax.axis_index("row"), lax.axis_index("col")
    z, core = row // 2, row % 2
    layers = N // 2
    sibling = (2 * z + 1 - core, col)
    early = z < layers // 2

    source = col // 4
    owner = row == source
    target = 4 * row + col // 4
    size = col_ref.shape[0]
    half = size // 2

    def piece(ref, index, rows):
        return ref.at[pl.ds(pl.multiple_of(index * rows, rows), rows), :]

    def wait_for(ref, sem):
        pltpu.make_async_copy(ref, ref, sem).wait()

    barrier = pltpu.get_barrier_semaphore()

    def greet(device):
        pl.semaphore_signal(barrier, inc=1, device_id=device, device_id_type=MESH)

    for i in range(1, layers):
        greet((2 * lax.rem(z + i, layers), col))
    for i in range(1, N):
        greet((2 * z + 1, lax.rem(col + i, N)))
    greet(sibling)

    own_rows = piece(row_ref, col, PANEL)
    pltpu.make_async_copy(diag_ref, piece(tile_ref, row, 8), tile_recv).start()

    @pl.when(target == col)
    def _():
        pltpu.make_async_copy(panel_ref, own_rows, top_recv).start()

    @pl.when(target != col)
    def _():
        pltpu.make_async_copy(panel_ref, own_rows, row_recv).start()

    def tell(sem):
        pl.semaphore_signal(sem, inc=1, device_id=sibling, device_id_type=MESH)

    def column_is_in():
        @pl.when(core == 0)
        def _():
            pl.semaphore_wait(barrier, N - 1)
            tell(row_ready)

        @pl.when(core == 1)
        def _():
            pl.semaphore_wait(row_ready, 1)

    def plane_is_in():
        @pl.when(core == 1)
        def _():
            pl.semaphore_wait(barrier, 2 * N - 1)
            tell(plane_ready)

        @pl.when(core == 0)
        def _():
            pl.semaphore_wait(plane_ready, 1)

    def send_tile():
        for i in range(1, N):
            pltpu.make_async_remote_copy(
                src_ref=diag_ref, dst_ref=piece(tile_ref, row, 8), send_sem=tile_send, recv_sem=tile_recv,
                device_id=(lax.rem(row + i, N), col), device_id_type=MESH,
            ).start()

    def send_rows(to, recv_sem):
        pltpu.make_async_remote_copy(
            src_ref=panel_ref, dst_ref=own_rows, send_sem=row_send, recv_sem=recv_sem,
            device_id=(row, to), device_id_type=MESH,
        ).start()

    @pl.when(jnp.logical_not(early))
    def _():
        column_is_in()
        send_tile()

    slab_copy = pltpu.make_async_copy(trailing_ref, slab_ref, slab_sem)
    slab_copy.start()
    plane_is_in()

    @pl.when((row < 4) & (target != col))
    def _():
        send_rows(target, top_recv)

    for i in range(1, N):
        to = lax.rem(col + i, N)

        @pl.when(to != target)
        def _():
            send_rows(to, row_recv)

    @pl.when(early)
    def _():
        column_is_in()
        send_tile()

    own_cols = piece(row_ref, col % 4, size)

    @pl.when(owner)
    def _():
        wait_for(own_cols, top_recv)
        for i in (1, 7, 2, 6, 3, 5, 4):
            for c in range(2):
                pltpu.make_async_remote_copy(
                    src_ref=piece(row_ref, 2 * (col % 4) + c, half), dst_ref=col_ref.at[pl.ds(c * half, half), :],
                    send_sem=half_send, recv_sem=half_recv.at[c],
                    device_id=(2 * lax.rem(z + i, layers) + c, col), device_id_type=MESH,
                ).start()
        for c in range(2):
            here, there = piece(row_ref, 2 * (col % 4) + c, half), col_ref.at[pl.ds(c * half, half), :]
            pltpu.make_async_remote_copy(
                src_ref=here, dst_ref=there, send_sem=half_send, recv_sem=half_recv.at[c],
                device_id=sibling, device_id_type=MESH,
            ).start()
            pltpu.make_async_copy(here, there, half_recv.at[c]).start()

    wait_for(tile_ref, tile_recv)

    my_half = piece(col_ref, core, half)
    passes = z != source // 2

    def between(k):
        if k != PASS_AT:
            return

        @pl.when(passes)
        def _():
            wait_for(my_half, half_recv.at[core])
            pltpu.make_async_remote_copy(
                src_ref=my_half, dst_ref=my_half, send_sem=pass_send, recv_sem=half_recv.at[core],
                device_id=sibling, device_id_type=MESH,
            ).start()

    invert_factor(tile_ref, inverse_ref, between)

    @pl.when(owner)
    def _():
        wait_for(row_ref.at[pl.ds(0, N * PANEL - size), :], row_recv)

    @pl.when(jnp.logical_not(owner))
    def _():
        wait_for(row_ref, row_recv)

    @pl.when(passes)
    def _():
        wait_for(piece(col_ref, 1 - core, half), half_recv.at[1 - core])
        wait_for(my_half, pass_send)

    @pl.when(jnp.logical_not(passes))
    def _():
        for c in range(2):
            wait_for(col_ref.at[pl.ds(c * half, half), :], half_recv.at[c])

    slab_copy.wait()
    wait_for(tile_ref.at[pl.ds(0, (N - 1) * 8), :], tile_send)
    wait_for(row_ref.at[pl.ds(0, (N - 1) * PANEL), :], row_send)

    @pl.when(owner)
    def _():
        for _ in range(N * half // row_ref.shape[0]):
            wait_for(row_ref, half_send)


def update_kernel(row_ref, col_ref, inverse_ref, slab_ref, solved_ref, updated_ref, out_ref, sems):
    row, col = lax.axis_index("row"), lax.axis_index("col")
    rows, cols = slab_ref.shape

    def solve(block):
        return lax.dot_general(
            block, inverse_ref[...], (((1,), (1,)), ((), ())), preferred_element_type=jnp.float32
        ).astype(jnp.bfloat16)

    solved_ref[...] = solve(row_ref[pl.ds(pl.multiple_of(col * PANEL, PANEL), PANEL), :])
    solved_cols = solve(col_ref[...])
    offset = row * rows - col * cols
    below = lax.broadcasted_iota(jnp.int32, (CHUNK, cols), 0) - lax.broadcasted_iota(jnp.int32, (CHUNK, cols), 1)
    copies = []
    for i in range(rows // CHUNK):
        part = pl.ds(i * CHUNK, CHUNK)
        solved_rows = solve(row_ref[part, :])
        change = lax.dot_general(
            solved_rows, solved_cols, (((1,), (1,)), ((), ())), preferred_element_type=jnp.float32
        )
        lower = below >= -(offset + i * CHUNK)
        old = slab_ref[part, :]
        out_ref[part, :] = jnp.where(lower, old - change, old)
        copy = pltpu.make_async_copy(out_ref.at[part, :], updated_ref.at[part, :], sems.at[i])
        copy.start()
        copies.append(copy)
    for copy in copies:
        copy.wait()


def per_device(diag_tile, panel, trailing):
    rows, cols = trailing.shape
    vmem = pl.BlockSpec(memory_space=pltpu.VMEM)
    hbm = pl.BlockSpec(memory_space=pltpu.HBM)
    dma = pltpu.SemaphoreType.DMA
    gathered = pl.pallas_call(
        gather_kernel,
        out_shape=(
            pltpu.VMEM((rows, PANEL), jnp.bfloat16),
            pltpu.VMEM((cols, PANEL), jnp.bfloat16),
            pltpu.VMEM((PANEL, PANEL), jnp.bfloat16),
            pltpu.VMEM((rows, cols), jnp.float32),
        ),
        in_specs=[hbm] * 3,
        out_specs=[vmem] * 4,
        scratch_shapes=[
            pltpu.VMEM((PANEL, PANEL), jnp.float32),
            dma(()),
            dma(()), dma(()), dma(()), dma(()), dma(()), dma(()), dma((2,)), dma(()),
            pltpu.SemaphoreType.REGULAR, pltpu.SemaphoreType.REGULAR,
        ],
        compiler_params=pltpu.CompilerParams(
            collective_id=0, has_side_effects=True, vmem_limit_bytes=16 << 20
        ),
        name="gather_and_factor",
    )(*[pltpu.with_memory_space_constraint(x, pltpu.HBM) for x in (diag_tile, panel, trailing)])
    return pl.pallas_call(
        update_kernel,
        out_shape=(
            jax.ShapeDtypeStruct((PANEL, PANEL), jnp.bfloat16),
            jax.ShapeDtypeStruct((rows, cols), jnp.float32),
        ),
        in_specs=[vmem] * 4,
        out_specs=[vmem, hbm],
        scratch_shapes=[pltpu.VMEM((rows, cols), jnp.float32), dma((rows // CHUNK,))],
        compiler_params=pltpu.CompilerParams(vmem_limit_bytes=24 << 20),
        name="solve_and_update",
    )(*[pltpu.with_memory_space_constraint(x, pltpu.VMEM) for x in gathered])


def solution(mesh):
    in_specs = (P("row", None), P(("row", "col"), None), P("row", "col"))
    out_specs = (P(("row", "col"), None), P("row", "col"))
    return jax.shard_map(
        per_device, mesh=mesh, in_specs=in_specs, out_specs=out_specs, check_vma=False
    )
```

```python
import functools

import jax
import jax.numpy as jnp
from jax import lax
from jax.experimental import pallas as pl
from jax.experimental.pallas import tpu as pltpu
from jax.sharding import PartitionSpec as P

MESH = pl.DeviceIdType.MESH
HIGHEST = lax.Precision.HIGHEST
N = 16
PANEL = 128
BLOCK = 32
PASS_AT = 2
CHUNK = 256


def spread(tile, sublane):
    return jnp.broadcast_to(tile[sublane : sublane + 1, :], (8, 128))


def eliminate(rows, k, lane, sub):
    tiles = BLOCK // 8
    first = BLOCK * k
    column = [
        [
            jnp.broadcast_to(rows[t][:, first + j : first + j + 1], (8, 128)) if t >= j // 8 else None
            for t in range(tiles)
        ]
        for j in range(BLOCK)
    ]
    in_block = (lane >= first) & (lane < first + BLOCK)
    packed = [
        jnp.where(in_block, jnp.where(lane - first == sub + 8 * t, 1.0, 0.0), rows[t]) for t in range(tiles)
    ]
    inverse_pivot = [None] * tiles
    for j in range(BLOCK):
        tj, sj = divmod(j, 8)
        r = 1.0 / spread(column[j][tj], sj)
        scaled = {t: column[j][t] * r for t in range(tj, tiles)}
        for m in range(j + 1, BLOCK):
            s = spread(column[j][m // 8], m % 8)
            for t in range(m // 8, tiles):
                column[m][t] = column[m][t] - scaled[t] * s
        row = spread(packed[tj], sj)
        for t in range(tj, tiles):
            if t == tj and sj == 7:
                continue
            factor = jnp.where(sub > sj, scaled[t], 0.0) if t == tj else scaled[t]
            packed[t] = packed[t] - factor * row
        inverse_pivot[tj] = r if inverse_pivot[tj] is None else jnp.where(sub == sj, r, inverse_pivot[tj])
    return packed, inverse_pivot


def invert_factor(tile_ref, inverse_ref, between):
    lane = lax.broadcasted_iota(jnp.int32, (8, 128), 1)
    sub = lax.broadcasted_iota(jnp.int32, (8, 128), 0)
    blocks, tiles = PANEL // BLOCK, BLOCK // 8
    for k in range(blocks):
        between(k)
        first, after = BLOCK * k, BLOCK * (k + 1)
        rows = [tile_ref[first + 8 * t : first + 8 * t + 8, :] for t in range(tiles)]
        packed, inverse_pivot = eliminate(rows, k, lane, sub)
        inverse = [
            jnp.where(lane < after, packed[t] * jnp.sqrt(inverse_pivot[t]), 0.0) for t in range(tiles)
        ]
        inverse_ref[first:after, :] = jnp.concatenate(inverse, axis=0).astype(jnp.bfloat16)
        if k < blocks - 1:
            left = jnp.concatenate(packed, axis=0).T[after:, :]
            right = jnp.concatenate([packed[t] * inverse_pivot[t] for t in range(tiles)], axis=0)
            change = lax.dot_general(
                left, right, (((1,), (0,)), ((), ())), precision=HIGHEST, preferred_element_type=jnp.float32
            )
            rest = tile_ref[after:, :]
            rest_lane = lax.broadcasted_iota(jnp.int32, rest.shape, 1)
            done = (rest_lane >= first) & (rest_lane < after)
            tile_ref[after:, :] = jnp.where(done, 0.0, rest) - change


def gather_kernel(
    diag_ref, panel_ref, trailing_ref,
    row_ref, col_ref, inverse_ref, slab_ref,
    tile_ref, slab_sem,
    tile_send, tile_recv, row_send, row_recv, top_recv, half_send, half_recv, pass_send,
    row_ready, plane_ready,
):
    row, col = lax.axis_index("row"), lax.axis_index("col")
    z, core = row // 2, row % 2
    layers = N // 2
    sibling = (2 * z + 1 - core, col)
    early = z < layers // 2

    source = col // 4
    owner = row == source
    target = 4 * row + col // 4
    size = col_ref.shape[0]
    half = size // 2

    def piece(ref, index, rows):
        return ref.at[pl.ds(pl.multiple_of(index * rows, rows), rows), :]

    def wait_for(ref, sem):
        pltpu.make_async_copy(ref, ref, sem).wait()

    barrier = pltpu.get_barrier_semaphore()

    def greet(device):
        pl.semaphore_signal(barrier, inc=1, device_id=device, device_id_type=MESH)

    for i in range(1, layers):
        greet((2 * lax.rem(z + i, layers), col))
    for i in range(1, N):
        greet((2 * z + 1, lax.rem(col + i, N)))
    greet(sibling)

    own_rows = piece(row_ref, col, PANEL)
    pltpu.make_async_copy(diag_ref, piece(tile_ref, row, 8), tile_recv).start()

    @pl.when(target == col)
    def _():
        pltpu.make_async_copy(panel_ref, own_rows, top_recv).start()

    @pl.when(target != col)
    def _():
        pltpu.make_async_copy(panel_ref, own_rows, row_recv).start()

    def tell(sem):
        pl.semaphore_signal(sem, inc=1, device_id=sibling, device_id_type=MESH)

    def column_is_in():
        @pl.when(core == 0)
        def _():
            pl.semaphore_wait(barrier, N - 1)
            tell(row_ready)

        @pl.when(core == 1)
        def _():
            pl.semaphore_wait(row_ready, 1)

    def plane_is_in():
        @pl.when(core == 1)
        def _():
            pl.semaphore_wait(barrier, 2 * N - 1)
            tell(plane_ready)

        @pl.when(core == 0)
        def _():
            pl.semaphore_wait(plane_ready, 1)

    def send_tile():
        for i in range(1, N):
            pltpu.make_async_remote_copy(
                src_ref=diag_ref, dst_ref=piece(tile_ref, row, 8), send_sem=tile_send, recv_sem=tile_recv,
                device_id=(lax.rem(row + i, N), col), device_id_type=MESH,
            ).start()

    def send_rows(to, recv_sem):
        pltpu.make_async_remote_copy(
            src_ref=panel_ref, dst_ref=own_rows, send_sem=row_send, recv_sem=recv_sem,
            device_id=(row, to), device_id_type=MESH,
        ).start()

    @pl.when(jnp.logical_not(early))
    def _():
        column_is_in()
        send_tile()

    slab_copy = pltpu.make_async_copy(trailing_ref, slab_ref, slab_sem)
    slab_copy.start()
    plane_is_in()

    @pl.when((row < 4) & (target != col))
    def _():
        send_rows(target, top_recv)

    @pl.when(early)
    def _():
        column_is_in()
        send_tile()

    for i in range(1, N):
        to = lax.rem(col + i, N)

        @pl.when(to != target)
        def _():
            send_rows(to, row_recv)

    own_cols = piece(row_ref, col % 4, size)

    @pl.when(owner)
    def _():
        wait_for(own_cols, top_recv)
        for i in (1, 7, 2, 6, 3, 5, 4):
            for c in range(2):
                pltpu.make_async_remote_copy(
                    src_ref=piece(row_ref, 2 * (col % 4) + c, half), dst_ref=col_ref.at[pl.ds(c * half, half), :],
                    send_sem=half_send, recv_sem=half_recv.at[c],
                    device_id=(2 * lax.rem(z + i, layers) + c, col), device_id_type=MESH,
                ).start()
        for c in range(2):
            here, there = piece(row_ref, 2 * (col % 4) + c, half), col_ref.at[pl.ds(c * half, half), :]
            pltpu.make_async_remote_copy(
                src_ref=here, dst_ref=there, send_sem=half_send, recv_sem=half_recv.at[c],
                device_id=sibling, device_id_type=MESH,
            ).start()
            pltpu.make_async_copy(here, there, half_recv.at[c]).start()

    wait_for(tile_ref, tile_recv)

    my_half = piece(col_ref, core, half)
    passes = z != source // 2

    def between(k):
        if k != PASS_AT:
            return

        @pl.when(passes)
        def _():
            wait_for(my_half, half_recv.at[core])
            pltpu.make_async_remote_copy(
                src_ref=my_half, dst_ref=my_half, send_sem=pass_send, recv_sem=half_recv.at[core],
                device_id=sibling, device_id_type=MESH,
            ).start()

    invert_factor(tile_ref, inverse_ref, between)

    @pl.when(owner)
    def _():
        wait_for(row_ref.at[pl.ds(0, N * PANEL - size), :], row_recv)

    @pl.when(jnp.logical_not(owner))
    def _():
        wait_for(row_ref, row_recv)

    @pl.when(passes)
    def _():
        wait_for(piece(col_ref, 1 - core, half), half_recv.at[1 - core])
        wait_for(my_half, pass_send)

    @pl.when(jnp.logical_not(passes))
    def _():
        for c in range(2):
            wait_for(col_ref.at[pl.ds(c * half, half), :], half_recv.at[c])

    slab_copy.wait()
    wait_for(tile_ref.at[pl.ds(0, (N - 1) * 8), :], tile_send)
    wait_for(row_ref.at[pl.ds(0, (N - 1) * PANEL), :], row_send)

    @pl.when(owner)
    def _():
        for _ in range(N * half // row_ref.shape[0]):
            wait_for(row_ref, half_send)


def update_kernel(row_ref, col_ref, inverse_ref, slab_ref, solved_ref, updated_ref, out_ref, sems):
    row, col = lax.axis_index("row"), lax.axis_index("col")
    rows, cols = slab_ref.shape

    def solve(block):
        return lax.dot_general(
            block, inverse_ref[...], (((1,), (1,)), ((), ())), preferred_element_type=jnp.float32
        ).astype(jnp.bfloat16)

    solved_ref[...] = solve(row_ref[pl.ds(pl.multiple_of(col * PANEL, PANEL), PANEL), :])
    solved_cols = solve(col_ref[...])
    offset = row * rows - col * cols
    below = lax.broadcasted_iota(jnp.int32, (CHUNK, cols), 0) - lax.broadcasted_iota(jnp.int32, (CHUNK, cols), 1)
    copies = []
    for i in range(rows // CHUNK):
        part = pl.ds(i * CHUNK, CHUNK)
        solved_rows = solve(row_ref[part, :])
        change = lax.dot_general(
            solved_rows, solved_cols, (((1,), (1,)), ((), ())), preferred_element_type=jnp.float32
        )
        lower = below >= -(offset + i * CHUNK)
        old = slab_ref[part, :]
        out_ref[part, :] = jnp.where(lower, old - change, old)
        copy = pltpu.make_async_copy(out_ref.at[part, :], updated_ref.at[part, :], sems.at[i])
        copy.start()
        copies.append(copy)
    for copy in copies:
        copy.wait()


def per_device(diag_tile, panel, trailing):
    rows, cols = trailing.shape
    vmem = pl.BlockSpec(memory_space=pltpu.VMEM)
    hbm = pl.BlockSpec(memory_space=pltpu.HBM)
    dma = pltpu.SemaphoreType.DMA
    gathered = pl.pallas_call(
        gather_kernel,
        out_shape=(
            pltpu.VMEM((rows, PANEL), jnp.bfloat16),
            pltpu.VMEM((cols, PANEL), jnp.bfloat16),
            pltpu.VMEM((PANEL, PANEL), jnp.bfloat16),
            pltpu.VMEM((rows, cols), jnp.float32),
        ),
        in_specs=[hbm] * 3,
        out_specs=[vmem] * 4,
        scratch_shapes=[
            pltpu.VMEM((PANEL, PANEL), jnp.float32),
            dma(()),
            dma(()), dma(()), dma(()), dma(()), dma(()), dma(()), dma((2,)), dma(()),
            pltpu.SemaphoreType.REGULAR, pltpu.SemaphoreType.REGULAR,
        ],
        compiler_params=pltpu.CompilerParams(
            collective_id=0, has_side_effects=True, vmem_limit_bytes=16 << 20
        ),
        name="gather_and_factor",
    )(*[pltpu.with_memory_space_constraint(x, pltpu.HBM) for x in (diag_tile, panel, trailing)])
    return pl.pallas_call(
        update_kernel,
        out_shape=(
            jax.ShapeDtypeStruct((PANEL, PANEL), jnp.bfloat16),
            jax.ShapeDtypeStruct((rows, cols), jnp.float32),
        ),
        in_specs=[vmem] * 4,
        out_specs=[vmem, hbm],
        scratch_shapes=[pltpu.VMEM((rows, cols), jnp.float32), dma((rows // CHUNK,))],
        compiler_params=pltpu.CompilerParams(vmem_limit_bytes=24 << 20),
        name="solve_and_update",
    )(*[pltpu.with_memory_space_constraint(x, pltpu.VMEM) for x in gathered])


def solution(mesh):
    in_specs = (P("row", None), P(("row", "col"), None), P("row", "col"))
    out_specs = (P(("row", "col"), None), P("row", "col"))
    return jax.shard_map(
        per_device, mesh=mesh, in_specs=in_specs, out_specs=out_specs, check_vma=False
    )
```

```python
import functools

import jax
import jax.numpy as jnp
from jax import lax
from jax.experimental import pallas as pl
from jax.experimental.pallas import tpu as pltpu
from jax.sharding import PartitionSpec as P

MESH = pl.DeviceIdType.MESH
HIGHEST = lax.Precision.HIGHEST
N = 16
PANEL = 128
BLOCK = 32
PASS_AT = 3
SOLVED = 512
CHUNK = 256


def spread(tile, sublane):
    return jnp.broadcast_to(tile[sublane : sublane + 1, :], (8, 128))


def eliminate(rows, k, lane, sub):
    tiles = BLOCK // 8
    first = BLOCK * k
    column = [
        [
            jnp.broadcast_to(rows[t][:, first + j : first + j + 1], (8, 128)) if t >= j // 8 else None
            for t in range(tiles)
        ]
        for j in range(BLOCK)
    ]
    in_block = (lane >= first) & (lane < first + BLOCK)
    packed = [
        jnp.where(in_block, jnp.where(lane - first == sub + 8 * t, 1.0, 0.0), rows[t]) for t in range(tiles)
    ]
    inverse_pivot = [None] * tiles
    for j in range(BLOCK):
        tj, sj = divmod(j, 8)
        r = 1.0 / spread(column[j][tj], sj)
        scaled = {t: column[j][t] * r for t in range(tj, tiles)}
        for m in range(j + 1, BLOCK):
            s = spread(column[j][m // 8], m % 8)
            for t in range(m // 8, tiles):
                column[m][t] = column[m][t] - scaled[t] * s
        row = spread(packed[tj], sj)
        for t in range(tj, tiles):
            if t == tj and sj == 7:
                continue
            factor = jnp.where(sub > sj, scaled[t], 0.0) if t == tj else scaled[t]
            packed[t] = packed[t] - factor * row
        inverse_pivot[tj] = r if inverse_pivot[tj] is None else jnp.where(sub == sj, r, inverse_pivot[tj])
    return packed, inverse_pivot


def invert_factor(tile_ref, inverse_ref, between):
    lane = lax.broadcasted_iota(jnp.int32, (8, 128), 1)
    sub = lax.broadcasted_iota(jnp.int32, (8, 128), 0)
    blocks, tiles = PANEL // BLOCK, BLOCK // 8
    for k in range(blocks):
        between(k)
        first, after = BLOCK * k, BLOCK * (k + 1)
        rows = [tile_ref[first + 8 * t : first + 8 * t + 8, :] for t in range(tiles)]
        packed, inverse_pivot = eliminate(rows, k, lane, sub)
        inverse = [
            jnp.where(lane < after, packed[t] * jnp.sqrt(inverse_pivot[t]), 0.0) for t in range(tiles)
        ]
        inverse_ref[first:after, :] = jnp.concatenate(inverse, axis=0).astype(jnp.bfloat16)
        if k < blocks - 1:
            left = jnp.concatenate(packed, axis=0).T[after:, :]
            right = jnp.concatenate([packed[t] * inverse_pivot[t] for t in range(tiles)], axis=0)
            change = lax.dot_general(
                left, right, (((1,), (0,)), ((), ())), precision=HIGHEST, preferred_element_type=jnp.float32
            )
            rest = tile_ref[after:, :]
            rest_lane = lax.broadcasted_iota(jnp.int32, rest.shape, 1)
            done = (rest_lane >= first) & (rest_lane < after)
            tile_ref[after:, :] = jnp.where(done, 0.0, rest) - change


def solve(rows, inverse):
    return lax.dot_general(
        rows, inverse, (((1,), (1,)), ((), ())), preferred_element_type=jnp.float32
    ).astype(jnp.bfloat16)


def gather_kernel(
    diag_ref, panel_ref, trailing_ref,
    solved_ref, col_ref, inverse_ref, slab_ref,
    tile_ref, row_ref, slab_sem,
    tile_send, tile_recv, row_send, row_recv, top_recv, half_send, half_recv, pass_send,
    row_ready, plane_ready,
):
    row, col = lax.axis_index("row"), lax.axis_index("col")
    z, core = row // 2, row % 2
    layers = N // 2
    sibling = (2 * z + 1 - core, col)
    early = z < layers // 2

    source = col // 4
    owner = row == source
    target = 4 * row + col // 4
    size = col_ref.shape[0]
    half = size // 2

    def piece(ref, index, rows):
        return ref.at[pl.ds(pl.multiple_of(index * rows, rows), rows), :]

    def wait_for(ref, sem):
        pltpu.make_async_copy(ref, ref, sem).wait()

    barrier = pltpu.get_barrier_semaphore()

    def greet(device):
        pl.semaphore_signal(barrier, inc=1, device_id=device, device_id_type=MESH)

    for i in range(1, layers):
        greet((2 * lax.rem(z + i, layers), col))
    for i in range(1, N):
        greet((2 * z + 1, lax.rem(col + i, N)))
    greet(sibling)

    own_rows = piece(row_ref, col, PANEL)
    pltpu.make_async_copy(diag_ref, piece(tile_ref, row, 8), tile_recv).start()

    @pl.when(target == col)
    def _():
        pltpu.make_async_copy(panel_ref, own_rows, top_recv).start()

    @pl.when(target != col)
    def _():
        pltpu.make_async_copy(panel_ref, own_rows, row_recv).start()

    def tell(sem):
        pl.semaphore_signal(sem, inc=1, device_id=sibling, device_id_type=MESH)

    def column_is_in():
        @pl.when(core == 0)
        def _():
            pl.semaphore_wait(barrier, N - 1)
            tell(row_ready)

        @pl.when(core == 1)
        def _():
            pl.semaphore_wait(row_ready, 1)

    def plane_is_in():
        @pl.when(core == 1)
        def _():
            pl.semaphore_wait(barrier, 2 * N - 1)
            tell(plane_ready)

        @pl.when(core == 0)
        def _():
            pl.semaphore_wait(plane_ready, 1)

    def send_tile():
        for i in range(1, N):
            pltpu.make_async_remote_copy(
                src_ref=diag_ref, dst_ref=piece(tile_ref, row, 8), send_sem=tile_send, recv_sem=tile_recv,
                device_id=(lax.rem(row + i, N), col), device_id_type=MESH,
            ).start()

    def send_rows(to, recv_sem):
        pltpu.make_async_remote_copy(
            src_ref=panel_ref, dst_ref=own_rows, send_sem=row_send, recv_sem=recv_sem,
            device_id=(row, to), device_id_type=MESH,
        ).start()

    @pl.when(jnp.logical_not(early))
    def _():
        column_is_in()
        send_tile()

    slab_copy = pltpu.make_async_copy(trailing_ref, slab_ref, slab_sem)
    slab_copy.start()
    plane_is_in()

    @pl.when((row < 4) & (target != col))
    def _():
        send_rows(target, top_recv)

    def send_some_rows(first, last):
        for i in range(first, last):
            to = lax.rem(col + i, N)

            @pl.when(to != target)
            def _():
                send_rows(to, row_recv)

    @pl.when(z >= 2)
    def _():
        send_some_rows(1, 16)

    @pl.when((z < 2) & (col >= 4))
    def _():
        send_some_rows(1, 8)

    @pl.when(early)
    def _():
        column_is_in()
        send_tile()

    @pl.when((z < 2) & (col >= 4))
    def _():
        send_some_rows(8, 16)

    @pl.when((z < 2) & (col < 4))
    def _():
        send_some_rows(1, 16)

    own_cols = piece(row_ref, col % 4, size)

    @pl.when(owner)
    def _():
        wait_for(own_cols, top_recv)
        for i in (1, 7, 2, 6, 3, 5, 4):
            for c in range(2):
                pltpu.make_async_remote_copy(
                    src_ref=piece(row_ref, 2 * (col % 4) + c, half), dst_ref=col_ref.at[pl.ds(c * half, half), :],
                    send_sem=half_send, recv_sem=half_recv.at[c],
                    device_id=(2 * lax.rem(z + i, layers) + c, col), device_id_type=MESH,
                ).start()
        for c in range(2):
            here, there = piece(row_ref, 2 * (col % 4) + c, half), col_ref.at[pl.ds(c * half, half), :]
            pltpu.make_async_remote_copy(
                src_ref=here, dst_ref=there, send_sem=half_send, recv_sem=half_recv.at[c],
                device_id=sibling, device_id_type=MESH,
            ).start()
            pltpu.make_async_copy(here, there, half_recv.at[c]).start()

    wait_for(tile_ref, tile_recv)

    my_half = piece(col_ref, core, half)
    passes = z != source // 2

    def between(k):
        if k != PASS_AT:
            return

        @pl.when(passes)
        def _():
            wait_for(my_half, half_recv.at[core])
            pltpu.make_async_remote_copy(
                src_ref=my_half, dst_ref=my_half, send_sem=pass_send, recv_sem=half_recv.at[core],
                device_id=sibling, device_id_type=MESH,
            ).start()

    invert_factor(tile_ref, inverse_ref, between)

    @pl.when(owner)
    def _():
        wait_for(row_ref.at[pl.ds(0, N * PANEL - size), :], row_recv)

    @pl.when(jnp.logical_not(owner))
    def _():
        wait_for(row_ref, row_recv)

    inverse = inverse_ref[...]
    for i in range(row_ref.shape[0] // SOLVED):
        part = pl.ds(i * SOLVED, SOLVED)
        solved_ref[part, :] = solve(row_ref[part, :], inverse)

    @pl.when(passes)
    def _():
        wait_for(piece(col_ref, 1 - core, half), half_recv.at[1 - core])
        wait_for(my_half, pass_send)

    @pl.when(jnp.logical_not(passes))
    def _():
        for c in range(2):
            wait_for(col_ref.at[pl.ds(c * half, half), :], half_recv.at[c])

    slab_copy.wait()
    wait_for(tile_ref.at[pl.ds(0, (N - 1) * 8), :], tile_send)
    wait_for(row_ref.at[pl.ds(0, (N - 1) * PANEL), :], row_send)

    @pl.when(owner)
    def _():
        for _ in range(N * half // row_ref.shape[0]):
            wait_for(row_ref, half_send)


def update_kernel(row_ref, col_ref, inverse_ref, slab_ref, solved_ref, updated_ref, out_ref, sems):
    row, col = lax.axis_index("row"), lax.axis_index("col")
    rows, cols = slab_ref.shape
    solved_ref[...] = row_ref[pl.ds(pl.multiple_of(col * PANEL, PANEL), PANEL), :]
    solved_cols = solve(col_ref[...], inverse_ref[...])
    offset = row * rows - col * cols
    below = lax.broadcasted_iota(jnp.int32, (CHUNK, cols), 0) - lax.broadcasted_iota(jnp.int32, (CHUNK, cols), 1)
    copies = []
    for i in range(rows // CHUNK):
        part = pl.ds(i * CHUNK, CHUNK)
        change = lax.dot_general(
            row_ref[part, :], solved_cols, (((1,), (1,)), ((), ())), preferred_element_type=jnp.float32
        )
        lower = below >= -(offset + i * CHUNK)
        old = slab_ref[part, :]
        out_ref[part, :] = jnp.where(lower, old - change, old)
        copy = pltpu.make_async_copy(out_ref.at[part, :], updated_ref.at[part, :], sems.at[i])
        copy.start()
        copies.append(copy)
    for copy in copies:
        copy.wait()


def per_device(diag_tile, panel, trailing):
    rows, cols = trailing.shape
    vmem = pl.BlockSpec(memory_space=pltpu.VMEM)
    hbm = pl.BlockSpec(memory_space=pltpu.HBM)
    dma = pltpu.SemaphoreType.DMA
    gathered = pl.pallas_call(
        gather_kernel,
        out_shape=(
            pltpu.VMEM((rows, PANEL), jnp.bfloat16),
            pltpu.VMEM((cols, PANEL), jnp.bfloat16),
            pltpu.VMEM((PANEL, PANEL), jnp.bfloat16),
            pltpu.VMEM((rows, cols), jnp.float32),
        ),
        in_specs=[hbm] * 3,
        out_specs=[vmem] * 4,
        scratch_shapes=[
            pltpu.VMEM((PANEL, PANEL), jnp.float32),
            pltpu.VMEM((rows, PANEL), jnp.bfloat16),
            dma(()),
            dma(()), dma(()), dma(()), dma(()), dma(()), dma(()), dma((2,)), dma(()),
            pltpu.SemaphoreType.REGULAR, pltpu.SemaphoreType.REGULAR,
        ],
        compiler_params=pltpu.CompilerParams(
            collective_id=0, has_side_effects=True, vmem_limit_bytes=16 << 20
        ),
        name="gather_and_factor",
    )(*[pltpu.with_memory_space_constraint(x, pltpu.HBM) for x in (diag_tile, panel, trailing)])
    return pl.pallas_call(
        update_kernel,
        out_shape=(
            jax.ShapeDtypeStruct((PANEL, PANEL), jnp.bfloat16),
            jax.ShapeDtypeStruct((rows, cols), jnp.float32),
        ),
        in_specs=[vmem] * 4,
        out_specs=[vmem, hbm],
        scratch_shapes=[pltpu.VMEM((rows, cols), jnp.float32), dma((rows // CHUNK,))],
        compiler_params=pltpu.CompilerParams(vmem_limit_bytes=24 << 20),
        name="solve_and_update",
    )(*[pltpu.with_memory_space_constraint(x, pltpu.VMEM) for x in gathered])


def solution(mesh):
    in_specs = (P("row", None), P(("row", "col"), None), P("row", "col"))
    out_specs = (P(("row", "col"), None), P("row", "col"))
    return jax.shard_map(
        per_device, mesh=mesh, in_specs=in_specs, out_specs=out_specs, check_vma=False
    )
```

```python
import functools

import jax
import jax.numpy as jnp
from jax import lax
from jax.experimental import pallas as pl
from jax.experimental.pallas import tpu as pltpu
from jax.sharding import PartitionSpec as P

MESH = pl.DeviceIdType.MESH
N = 16
PANEL = 128
BLOCK = 16
PASS_AT = 7
SOLVED = 512
CHUNK = 256


def spread(tile, sublane):
    return jnp.broadcast_to(tile[sublane : sublane + 1, :], (8, 128))


def split(x):
    high = x.astype(jnp.bfloat16)
    x = x - high.astype(jnp.float32)
    middle = x.astype(jnp.bfloat16)
    return high, middle, (x - middle.astype(jnp.float32)).astype(jnp.bfloat16)


def outer(left, right):
    h, m, l = split(left)
    high, middle, low = split(right)
    return lax.dot_general(
        jnp.concatenate([l, m, h, m, h, h], axis=0),
        jnp.concatenate([high, middle, low, high, middle, high], axis=0),
        (((0,), (0,)), ((), ())),
        preferred_element_type=jnp.float32,
    )


def invert_factor(tile_ref, inverse_ref, between):
    lane = lax.broadcasted_iota(jnp.int32, (8, 128), 1)
    sub = lax.broadcasted_iota(jnp.int32, (8, 128), 0)
    tiles, total = BLOCK // 8, PANEL // 8
    held = [tile_ref[8 * i : 8 * i + 8, :] for i in range(total)]
    for k in range(PANEL // BLOCK):
        between(k)
        first, base = BLOCK * k, tiles * k
        count = min(2 * tiles, total - base)
        rows = held[base : base + count]
        column = [
            [
                jnp.broadcast_to(rows[t][:, first + j : first + j + 1], (8, 128)) if t >= j // 8 else None
                for t in range(count)
            ]
            for j in range(BLOCK)
        ]
        in_block = (lane >= first) & (lane < first + BLOCK)
        packed = [
            jnp.where(in_block, jnp.where(lane - first == sub + 8 * t, 1.0, 0.0) if t < tiles else 0.0, rows[t])
            for t in range(count)
        ]
        inverse_pivot = [None] * tiles
        for j in range(BLOCK):
            tj, sj = divmod(j, 8)
            r = 1.0 / spread(column[j][tj], sj)
            scaled = {t: column[j][t] * r for t in range(tj, count)}
            for m in range(j + 1, BLOCK):
                s = spread(column[j][m // 8], m % 8)
                for t in range(m // 8, count):
                    column[m][t] = column[m][t] - scaled[t] * s
            row = spread(packed[tj], sj)
            for t in range(tj, count):
                if t == tj and sj == 7:
                    continue
                factor = jnp.where(sub > sj, scaled[t], 0.0) if t == tj else scaled[t]
                packed[t] = packed[t] - factor * row
            inverse_pivot[tj] = r if inverse_pivot[tj] is None else jnp.where(sub == sj, r, inverse_pivot[tj])
        inverse = [
            jnp.where(lane < first + BLOCK, packed[t] * jnp.sqrt(inverse_pivot[t]), 0.0) for t in range(tiles)
        ]
        inverse_ref[first : first + BLOCK, :] = jnp.concatenate(inverse, axis=0).astype(jnp.bfloat16)
        held[base + tiles : base + count] = packed[tiles:]
        if base + 2 * tiles < total:
            change = outer(
                jnp.concatenate(packed[:tiles], axis=0),
                jnp.concatenate([packed[t] * inverse_pivot[t] for t in range(tiles)], axis=0),
            )
            for i in range(base + 2 * tiles, total):
                held[i] = jnp.where(in_block, 0.0, held[i]) - change[8 * i : 8 * i + 8, :]


def solve(rows, inverse):
    return lax.dot_general(
        rows, inverse, (((1,), (1,)), ((), ())), preferred_element_type=jnp.float32
    ).astype(jnp.bfloat16)


def gather_kernel(
    diag_ref, panel_ref, trailing_ref,
    solved_ref, col_ref, inverse_ref, slab_ref,
    tile_ref, row_ref, slab_sem,
    tile_send, tile_recv, row_send, row_recv, top_recv, half_send, half_recv, pass_send,
    row_ready, plane_ready,
):
    row, col = lax.axis_index("row"), lax.axis_index("col")
    z, core = row // 2, row % 2
    layers = N // 2
    sibling = (2 * z + 1 - core, col)
    early = z < layers // 2

    source = col // 4
    owner = row == source
    target = 4 * row + col // 4
    size = col_ref.shape[0]
    half = size // 2

    def piece(ref, index, rows):
        return ref.at[pl.ds(pl.multiple_of(index * rows, rows), rows), :]

    def wait_for(ref, sem):
        pltpu.make_async_copy(ref, ref, sem).wait()

    barrier = pltpu.get_barrier_semaphore()

    def greet(device):
        pl.semaphore_signal(barrier, inc=1, device_id=device, device_id_type=MESH)

    for i in range(1, layers):
        greet((2 * lax.rem(z + i, layers), col))
    for i in range(1, N):
        greet((2 * z + 1, lax.rem(col + i, N)))
    greet(sibling)

    own_rows = piece(row_ref, col, PANEL)
    pltpu.make_async_copy(diag_ref, piece(tile_ref, row, 8), tile_recv).start()

    @pl.when(target == col)
    def _():
        pltpu.make_async_copy(panel_ref, own_rows, top_recv).start()

    @pl.when(target != col)
    def _():
        pltpu.make_async_copy(panel_ref, own_rows, row_recv).start()

    def tell(sem):
        pl.semaphore_signal(sem, inc=1, device_id=sibling, device_id_type=MESH)

    def column_is_in():
        @pl.when(core == 0)
        def _():
            pl.semaphore_wait(barrier, N - 1)
            tell(row_ready)

        @pl.when(core == 1)
        def _():
            pl.semaphore_wait(row_ready, 1)

    def plane_is_in():
        @pl.when(core == 1)
        def _():
            pl.semaphore_wait(barrier, 2 * N - 1)
            tell(plane_ready)

        @pl.when(core == 0)
        def _():
            pl.semaphore_wait(plane_ready, 1)

    def send_tile():
        for i in range(1, N):
            pltpu.make_async_remote_copy(
                src_ref=diag_ref, dst_ref=piece(tile_ref, row, 8), send_sem=tile_send, recv_sem=tile_recv,
                device_id=(lax.rem(row + i, N), col), device_id_type=MESH,
            ).start()

    def send_rows(to, recv_sem):
        pltpu.make_async_remote_copy(
            src_ref=panel_ref, dst_ref=own_rows, send_sem=row_send, recv_sem=recv_sem,
            device_id=(row, to), device_id_type=MESH,
        ).start()

    @pl.when(jnp.logical_not(early))
    def _():
        column_is_in()
        send_tile()

    slab_copy = pltpu.make_async_copy(trailing_ref, slab_ref, slab_sem)
    slab_copy.start()
    plane_is_in()

    @pl.when((row < 4) & (target != col))
    def _():
        send_rows(target, top_recv)

    def send_some_rows(first, last):
        for i in range(first, last):
            to = lax.rem(col + i, N)

            @pl.when(to != target)
            def _():
                send_rows(to, row_recv)

    @pl.when(z >= 2)
    def _():
        send_some_rows(1, 16)

    @pl.when((z < 2) & (col >= 4))
    def _():
        send_some_rows(1, 8)

    @pl.when(early)
    def _():
        column_is_in()
        send_tile()

    @pl.when((z < 2) & (col >= 4))
    def _():
        send_some_rows(8, 16)

    @pl.when((z < 2) & (col < 4))
    def _():
        send_some_rows(1, 16)

    own_cols = piece(row_ref, col % 4, size)

    @pl.when(owner)
    def _():
        wait_for(own_cols, top_recv)
        for i in (1, 7, 2, 6, 3 + z, 5, 4 - z):
            for c in range(2):
                pltpu.make_async_remote_copy(
                    src_ref=piece(row_ref, 2 * (col % 4) + c, half), dst_ref=col_ref.at[pl.ds(c * half, half), :],
                    send_sem=half_send, recv_sem=half_recv.at[c],
                    device_id=(2 * lax.rem(z + i, layers) + c, col), device_id_type=MESH,
                ).start()
        for c in range(2):
            here, there = piece(row_ref, 2 * (col % 4) + c, half), col_ref.at[pl.ds(c * half, half), :]
            pltpu.make_async_remote_copy(
                src_ref=here, dst_ref=there, send_sem=half_send, recv_sem=half_recv.at[c],
                device_id=sibling, device_id_type=MESH,
            ).start()
            pltpu.make_async_copy(here, there, half_recv.at[c]).start()

    wait_for(tile_ref, tile_recv)

    my_half = piece(col_ref, core, half)
    passes = z != source // 2

    def between(k):
        if k != PASS_AT:
            return

        @pl.when(passes)
        def _():
            wait_for(my_half, half_recv.at[core])
            pltpu.make_async_remote_copy(
                src_ref=my_half, dst_ref=my_half, send_sem=pass_send, recv_sem=half_recv.at[core],
                device_id=sibling, device_id_type=MESH,
            ).start()

    invert_factor(tile_ref, inverse_ref, between)

    @pl.when(owner)
    def _():
        wait_for(row_ref.at[pl.ds(0, N * PANEL - size), :], row_recv)

    @pl.when(jnp.logical_not(owner))
    def _():
        wait_for(row_ref, row_recv)

    inverse = inverse_ref[...]
    for i in range(row_ref.shape[0] // SOLVED):
        part = pl.ds(i * SOLVED, SOLVED)
        solved_ref[part, :] = solve(row_ref[part, :], inverse)

    @pl.when(passes)
    def _():
        wait_for(piece(col_ref, 1 - core, half), half_recv.at[1 - core])
        wait_for(my_half, pass_send)

    @pl.when(jnp.logical_not(passes))
    def _():
        for c in range(2):
            wait_for(col_ref.at[pl.ds(c * half, half), :], half_recv.at[c])

    slab_copy.wait()
    wait_for(tile_ref.at[pl.ds(0, (N - 1) * 8), :], tile_send)
    wait_for(row_ref.at[pl.ds(0, (N - 1) * PANEL), :], row_send)

    @pl.when(owner)
    def _():
        for _ in range(N * half // row_ref.shape[0]):
            wait_for(row_ref, half_send)


def update_kernel(row_ref, col_ref, inverse_ref, slab_ref, solved_ref, updated_ref, out_ref, sems):
    row, col = lax.axis_index("row"), lax.axis_index("col")
    rows, cols = slab_ref.shape
    solved_ref[...] = row_ref[pl.ds(pl.multiple_of(col * PANEL, PANEL), PANEL), :]
    solved_cols = solve(col_ref[...], inverse_ref[...])
    offset = row * rows - col * cols
    below = lax.broadcasted_iota(jnp.int32, (CHUNK, cols), 0) - lax.broadcasted_iota(jnp.int32, (CHUNK, cols), 1)
    copies = []
    for i in range(rows // CHUNK):
        part = pl.ds(i * CHUNK, CHUNK)
        change = lax.dot_general(
            row_ref[part, :], solved_cols, (((1,), (1,)), ((), ())), preferred_element_type=jnp.float32
        )
        lower = below >= -(offset + i * CHUNK)
        old = slab_ref[part, :]
        out_ref[part, :] = jnp.where(lower, old - change, old)
        copy = pltpu.make_async_copy(out_ref.at[part, :], updated_ref.at[part, :], sems.at[i])
        copy.start()
        copies.append(copy)
    for copy in copies:
        copy.wait()


def per_device(diag_tile, panel, trailing):
    rows, cols = trailing.shape
    vmem = pl.BlockSpec(memory_space=pltpu.VMEM)
    hbm = pl.BlockSpec(memory_space=pltpu.HBM)
    dma = pltpu.SemaphoreType.DMA
    gathered = pl.pallas_call(
        gather_kernel,
        out_shape=(
            pltpu.VMEM((rows, PANEL), jnp.bfloat16),
            pltpu.VMEM((cols, PANEL), jnp.bfloat16),
            pltpu.VMEM((PANEL, PANEL), jnp.bfloat16),
            pltpu.VMEM((rows, cols), jnp.float32),
        ),
        in_specs=[hbm] * 3,
        out_specs=[vmem] * 4,
        scratch_shapes=[
            pltpu.VMEM((PANEL, PANEL), jnp.float32),
            pltpu.VMEM((rows, PANEL), jnp.bfloat16),
            dma(()),
            dma(()), dma(()), dma(()), dma(()), dma(()), dma(()), dma((2,)), dma(()),
            pltpu.SemaphoreType.REGULAR, pltpu.SemaphoreType.REGULAR,
        ],
        compiler_params=pltpu.CompilerParams(
            collective_id=0, has_side_effects=True, vmem_limit_bytes=16 << 20
        ),
        name="gather_and_factor",
    )(*[pltpu.with_memory_space_constraint(x, pltpu.HBM) for x in (diag_tile, panel, trailing)])
    return pl.pallas_call(
        update_kernel,
        out_shape=(
            jax.ShapeDtypeStruct((PANEL, PANEL), jnp.bfloat16),
            jax.ShapeDtypeStruct((rows, cols), jnp.float32),
        ),
        in_specs=[vmem] * 4,
        out_specs=[vmem, hbm],
        scratch_shapes=[pltpu.VMEM((rows, cols), jnp.float32), dma((rows // CHUNK,))],
        compiler_params=pltpu.CompilerParams(vmem_limit_bytes=24 << 20),
        name="solve_and_update",
    )(*[pltpu.with_memory_space_constraint(x, pltpu.VMEM) for x in gathered])


def solution(mesh):
    in_specs = (P("row", None), P(("row", "col"), None), P("row", "col"))
    out_specs = (P(("row", "col"), None), P("row", "col"))
    return jax.shard_map(
        per_device, mesh=mesh, in_specs=in_specs, out_specs=out_specs, check_vma=False
    )
```

```python
import functools

import jax
import jax.numpy as jnp
from jax import lax
from jax.experimental import pallas as pl
from jax.experimental.pallas import tpu as pltpu
from jax.sharding import PartitionSpec as P

MESH = pl.DeviceIdType.MESH
N = 16
PANEL = 128
BLOCK = 16
PASS_AT = 7
SOLVED = 512
CHUNK = 256


def spread(tile, sublane):
    return jnp.broadcast_to(tile[sublane : sublane + 1, :], (8, 128))


def split(x):
    high = x.astype(jnp.bfloat16)
    x = x - high.astype(jnp.float32)
    middle = x.astype(jnp.bfloat16)
    return high, middle, (x - middle.astype(jnp.float32)).astype(jnp.bfloat16)


def outer(left, right):
    h, m, l = split(left)
    high, middle, low = split(right)
    return lax.dot_general(
        jnp.concatenate([l, m, h, m, h, h], axis=0),
        jnp.concatenate([high, middle, low, high, middle, high], axis=0),
        (((0,), (0,)), ((), ())),
        preferred_element_type=jnp.float32,
    )


def invert_factor(tile_ref, inverse_ref, between):
    lane = lax.broadcasted_iota(jnp.int32, (8, 128), 1)
    sub = lax.broadcasted_iota(jnp.int32, (8, 128), 0)
    tiles, total = BLOCK // 8, PANEL // 8
    held = [tile_ref[8 * i : 8 * i + 8, :] for i in range(total)]
    for k in range(PANEL // BLOCK):
        between(k)
        first, base = BLOCK * k, tiles * k
        count = min(2 * tiles, total - base)
        rows = held[base : base + count]
        column = [
            [
                jnp.broadcast_to(rows[t][:, first + j : first + j + 1], (8, 128)) if t >= j // 8 else None
                for t in range(count)
            ]
            for j in range(BLOCK)
        ]
        in_block = (lane >= first) & (lane < first + BLOCK)
        packed = [
            jnp.where(in_block, jnp.where(lane - first == sub + 8 * t, 1.0, 0.0) if t < tiles else 0.0, rows[t])
            for t in range(count)
        ]
        inverse_pivot = [None] * tiles
        for j in range(BLOCK):
            tj, sj = divmod(j, 8)
            r = 1.0 / spread(column[j][tj], sj)
            scaled = {t: column[j][t] * r for t in range(tj, count)}
            for m in range(j + 1, BLOCK):
                s = spread(column[j][m // 8], m % 8)
                for t in range(m // 8, count):
                    column[m][t] = column[m][t] - scaled[t] * s
            row = spread(packed[tj], sj)
            for t in range(tj, count):
                if t == tj and sj == 7:
                    continue
                factor = jnp.where(sub > sj, scaled[t], 0.0) if t == tj else scaled[t]
                packed[t] = packed[t] - factor * row
            inverse_pivot[tj] = r if inverse_pivot[tj] is None else jnp.where(sub == sj, r, inverse_pivot[tj])
        inverse = [
            jnp.where(lane < first + BLOCK, packed[t] * jnp.sqrt(inverse_pivot[t]), 0.0) for t in range(tiles)
        ]
        inverse_ref[first : first + BLOCK, :] = jnp.concatenate(inverse, axis=0).astype(jnp.bfloat16)
        held[base + tiles : base + count] = packed[tiles:]
        if base + 2 * tiles < total:
            change = outer(
                jnp.concatenate(packed[:tiles], axis=0),
                jnp.concatenate([packed[t] * inverse_pivot[t] for t in range(tiles)], axis=0),
            )
            for i in range(base + 2 * tiles, total):
                held[i] = jnp.where(in_block, 0.0, held[i]) - change[8 * i : 8 * i + 8, :]


def solve(rows, inverse):
    return lax.dot_general(
        rows, inverse, (((1,), (1,)), ((), ())), preferred_element_type=jnp.float32
    ).astype(jnp.bfloat16)


def gather_kernel(
    diag_ref, panel_ref, trailing_ref,
    solved_ref, col_ref, inverse_ref, slab_ref,
    tile_ref, row_ref, slab_sem,
    tile_send, tile_recv, row_send, row_recv, top_recv, half_send, half_recv, pass_send,
    row_ready, plane_ready,
):
    row, col = lax.axis_index("row"), lax.axis_index("col")
    z, core = row // 2, row % 2
    layers = N // 2
    sibling = (2 * z + 1 - core, col)
    early = z < layers // 2

    source = col // 4
    owner = row == source
    target = 4 * row + col // 4
    size = col_ref.shape[0]
    half = size // 2

    def piece(ref, index, rows):
        return ref.at[pl.ds(pl.multiple_of(index * rows, rows), rows), :]

    def wait_for(ref, sem):
        pltpu.make_async_copy(ref, ref, sem).wait()

    barrier = pltpu.get_barrier_semaphore()

    def greet(device):
        pl.semaphore_signal(barrier, inc=1, device_id=device, device_id_type=MESH)

    for i in range(1, layers):
        greet((2 * lax.rem(z + i, layers), col))
    for i in range(1, N):
        greet((2 * z + 1, lax.rem(col + i, N)))
    greet(sibling)

    own_rows = piece(row_ref, col, PANEL)
    pltpu.make_async_copy(diag_ref, piece(tile_ref, row, 8), tile_recv).start()

    @pl.when(target == col)
    def _():
        pltpu.make_async_copy(panel_ref, own_rows, top_recv).start()

    @pl.when(target != col)
    def _():
        pltpu.make_async_copy(panel_ref, own_rows, row_recv).start()

    def tell(sem):
        pl.semaphore_signal(sem, inc=1, device_id=sibling, device_id_type=MESH)

    def column_is_in():
        @pl.when(core == 0)
        def _():
            pl.semaphore_wait(barrier, N - 1)
            tell(row_ready)

        @pl.when(core == 1)
        def _():
            pl.semaphore_wait(row_ready, 1)

    def plane_is_in():
        @pl.when(core == 1)
        def _():
            pl.semaphore_wait(barrier, 2 * N - 1)
            tell(plane_ready)

        @pl.when(core == 0)
        def _():
            pl.semaphore_wait(plane_ready, 1)

    def send_tile():
        for i in (8, 7, 9, 6, 10, 5, 11, 4, 12, 3, 13, 2, 14, 1, 15):
            pltpu.make_async_remote_copy(
                src_ref=diag_ref, dst_ref=piece(tile_ref, row, 8), send_sem=tile_send, recv_sem=tile_recv,
                device_id=(lax.rem(row + i, N), col), device_id_type=MESH,
            ).start()

    def send_rows(to, recv_sem):
        pltpu.make_async_remote_copy(
            src_ref=panel_ref, dst_ref=own_rows, send_sem=row_send, recv_sem=recv_sem,
            device_id=(row, to), device_id_type=MESH,
        ).start()

    @pl.when(jnp.logical_not(early))
    def _():
        column_is_in()
        send_tile()

    slab_copy = pltpu.make_async_copy(trailing_ref, slab_ref, slab_sem)
    slab_copy.start()
    plane_is_in()

    @pl.when((row < 4) & (target != col))
    def _():
        send_rows(target, top_recv)

    def send_some_rows(first, last):
        for i in range(first, last):
            to = lax.rem(col + i, N)

            @pl.when(to != target)
            def _():
                send_rows(to, row_recv)

    @pl.when(z >= 2)
    def _():
        send_some_rows(1, 16)

    @pl.when((z < 2) & (col >= 4))
    def _():
        send_some_rows(1, 8)

    @pl.when(early)
    def _():
        column_is_in()
        send_tile()

    @pl.when((z < 2) & (col >= 4))
    def _():
        send_some_rows(8, 16)

    @pl.when((z < 2) & (col < 4))
    def _():
        send_some_rows(1, 16)

    own_cols = piece(row_ref, col % 4, size)

    def quarter(p):
        return piece(col_ref, p, PANEL)


    @pl.when(owner)
    def _():
        wait_for(own_cols, top_recv)
        for i in (1, 7, 2, 6, 3 + z, 5, 4 - z):
            for p in range(4):
                pltpu.make_async_remote_copy(
                    src_ref=piece(row_ref, 4 * (col % 4) + p, PANEL), dst_ref=quarter(p),
                    send_sem=half_send, recv_sem=half_recv.at[p],
                    device_id=(2 * lax.rem(z + i, layers) + p // 2, col), device_id_type=MESH,
                ).start()
        for p in range(4):
            here = piece(row_ref, 4 * (col % 4) + p, PANEL)
            pltpu.make_async_remote_copy(
                src_ref=here, dst_ref=quarter(p), send_sem=half_send, recv_sem=half_recv.at[p],
                device_id=sibling, device_id_type=MESH,
            ).start()
            pltpu.make_async_copy(here, quarter(p), half_recv.at[p]).start()

    wait_for(tile_ref, tile_recv)

    my_half = piece(col_ref, core, half)
    passes = z != source // 2

    def between(k):
        if k != PASS_AT:
            return

        @pl.when(passes)
        def _():
            for i in range(2):
                p = 2 * core + i
                wait_for(quarter(p), half_recv.at[p])
                pltpu.make_async_remote_copy(
                    src_ref=quarter(p), dst_ref=quarter(p), send_sem=pass_send, recv_sem=half_recv.at[p],
                    device_id=sibling, device_id_type=MESH,
                ).start()

    invert_factor(tile_ref, inverse_ref, between)

    @pl.when(owner)
    def _():
        wait_for(row_ref.at[pl.ds(0, N * PANEL - size), :], row_recv)

    @pl.when(jnp.logical_not(owner))
    def _():
        wait_for(row_ref, row_recv)

    inverse = inverse_ref[...]
    for i in range(row_ref.shape[0] // SOLVED):
        part = pl.ds(i * SOLVED, SOLVED)
        solved_ref[part, :] = solve(row_ref[part, :], inverse)

    @pl.when(passes)
    def _():
        for i in range(2):
            p = 2 * (1 - core) + i
            wait_for(quarter(p), half_recv.at[p])
        wait_for(my_half, pass_send)

    @pl.when(jnp.logical_not(passes))
    def _():
        for p in range(4):
            wait_for(quarter(p), half_recv.at[p])

    slab_copy.wait()
    wait_for(tile_ref.at[pl.ds(0, (N - 1) * 8), :], tile_send)
    wait_for(row_ref.at[pl.ds(0, (N - 1) * PANEL), :], row_send)

    @pl.when(owner)
    def _():
        for _ in range(N * half // row_ref.shape[0]):
            wait_for(row_ref, half_send)


def update_kernel(row_ref, col_ref, inverse_ref, slab_ref, solved_ref, updated_ref, out_ref, sems):
    row, col = lax.axis_index("row"), lax.axis_index("col")
    rows, cols = slab_ref.shape
    solved_ref[...] = row_ref[pl.ds(pl.multiple_of(col * PANEL, PANEL), PANEL), :]
    solved_cols = solve(col_ref[...], inverse_ref[...])
    offset = row * rows - col * cols
    below = lax.broadcasted_iota(jnp.int32, (CHUNK, cols), 0) - lax.broadcasted_iota(jnp.int32, (CHUNK, cols), 1)
    copies = []
    for i in range(rows // CHUNK):
        part = pl.ds(i * CHUNK, CHUNK)
        change = lax.dot_general(
            row_ref[part, :], solved_cols, (((1,), (1,)), ((), ())), preferred_element_type=jnp.float32
        )
        lower = below >= -(offset + i * CHUNK)
        old = slab_ref[part, :]
        out_ref[part, :] = jnp.where(lower, old - change, old)
        copy = pltpu.make_async_copy(out_ref.at[part, :], updated_ref.at[part, :], sems.at[i])
        copy.start()
        copies.append(copy)
    for copy in copies:
        copy.wait()


def per_device(diag_tile, panel, trailing):
    rows, cols = trailing.shape
    vmem = pl.BlockSpec(memory_space=pltpu.VMEM)
    hbm = pl.BlockSpec(memory_space=pltpu.HBM)
    dma = pltpu.SemaphoreType.DMA
    gathered = pl.pallas_call(
        gather_kernel,
        out_shape=(
            pltpu.VMEM((rows, PANEL), jnp.bfloat16),
            pltpu.VMEM((cols, PANEL), jnp.bfloat16),
            pltpu.VMEM((PANEL, PANEL), jnp.bfloat16),
            pltpu.VMEM((rows, cols), jnp.float32),
        ),
        in_specs=[hbm] * 3,
        out_specs=[vmem] * 4,
        scratch_shapes=[
            pltpu.VMEM((PANEL, PANEL), jnp.float32),
            pltpu.VMEM((rows, PANEL), jnp.bfloat16),
            dma(()),
            dma(()), dma(()), dma(()), dma(()), dma(()), dma(()), dma((4,)), dma(()),
            pltpu.SemaphoreType.REGULAR, pltpu.SemaphoreType.REGULAR,
        ],
        compiler_params=pltpu.CompilerParams(
            collective_id=0, has_side_effects=True, vmem_limit_bytes=16 << 20
        ),
        name="gather_and_factor",
    )(*[pltpu.with_memory_space_constraint(x, pltpu.HBM) for x in (diag_tile, panel, trailing)])
    return pl.pallas_call(
        update_kernel,
        out_shape=(
            jax.ShapeDtypeStruct((PANEL, PANEL), jnp.bfloat16),
            jax.ShapeDtypeStruct((rows, cols), jnp.float32),
        ),
        in_specs=[vmem] * 4,
        out_specs=[vmem, hbm],
        scratch_shapes=[pltpu.VMEM((rows, cols), jnp.float32), dma((rows // CHUNK,))],
        compiler_params=pltpu.CompilerParams(vmem_limit_bytes=24 << 20),
        name="solve_and_update",
    )(*[pltpu.with_memory_space_constraint(x, pltpu.VMEM) for x in gathered])


def solution(mesh):
    in_specs = (P("row", None), P(("row", "col"), None), P("row", "col"))
    out_specs = (P(("row", "col"), None), P("row", "col"))
    return jax.shard_map(
        per_device, mesh=mesh, in_specs=in_specs, out_specs=out_specs, check_vma=False
    )
```

```python
import functools

import jax
import jax.numpy as jnp
from jax import lax
from jax.experimental import pallas as pl
from jax.experimental.pallas import tpu as pltpu
from jax.sharding import PartitionSpec as P

MESH = pl.DeviceIdType.MESH
N = 16
PANEL = 128
BLOCK = 16
PASS_AT = 7
SOLVED = 512
CHUNK = 256


def spread(tile, sublane):
    return jnp.broadcast_to(tile[sublane : sublane + 1, :], (8, 128))


def split(x):
    high = x.astype(jnp.bfloat16)
    x = x - high.astype(jnp.float32)
    middle = x.astype(jnp.bfloat16)
    return high, middle, (x - middle.astype(jnp.float32)).astype(jnp.bfloat16)


def outer(left, right):
    h, m, l = split(left)
    high, middle, low = split(right)
    return lax.dot_general(
        jnp.concatenate([l, m, h, m, h, h], axis=0),
        jnp.concatenate([high, middle, low, high, middle, high], axis=0),
        (((0,), (0,)), ((), ())),
        preferred_element_type=jnp.float32,
    )


def invert_factor(tile_ref, inverse_ref, between):
    lane = lax.broadcasted_iota(jnp.int32, (8, 128), 1)
    sub = lax.broadcasted_iota(jnp.int32, (8, 128), 0)
    tiles, total = BLOCK // 8, PANEL // 8
    held = [tile_ref[8 * i : 8 * i + 8, :] for i in range(total)]
    for k in range(PANEL // BLOCK):
        between(k)
        first, base = BLOCK * k, tiles * k
        count = min(2 * tiles, total - base)
        rows = held[base : base + count]
        column = [
            [
                jnp.broadcast_to(rows[t][:, first + j : first + j + 1], (8, 128)) if t >= j // 8 else None
                for t in range(count)
            ]
            for j in range(BLOCK)
        ]
        in_block = (lane >= first) & (lane < first + BLOCK)
        packed = [
            jnp.where(in_block, jnp.where(lane - first == sub + 8 * t, 1.0, 0.0) if t < tiles else 0.0, rows[t])
            for t in range(count)
        ]
        inverse_pivot = [None] * tiles
        for j in range(BLOCK):
            tj, sj = divmod(j, 8)
            r = 1.0 / spread(column[j][tj], sj)
            scaled = {t: column[j][t] * r for t in range(tj, count)}
            for m in range(j + 1, BLOCK):
                s = spread(column[j][m // 8], m % 8)
                for t in range(m // 8, count):
                    column[m][t] = column[m][t] - scaled[t] * s
            row = spread(packed[tj], sj)
            for t in range(tj, count):
                if t == tj and sj == 7:
                    continue
                factor = jnp.where(sub > sj, scaled[t], 0.0) if t == tj else scaled[t]
                packed[t] = packed[t] - factor * row
            inverse_pivot[tj] = r if inverse_pivot[tj] is None else jnp.where(sub == sj, r, inverse_pivot[tj])
        inverse = [
            jnp.where(lane < first + BLOCK, packed[t] * jnp.sqrt(inverse_pivot[t]), 0.0) for t in range(tiles)
        ]
        inverse_ref[first : first + BLOCK, :] = jnp.concatenate(inverse, axis=0).astype(jnp.bfloat16)
        held[base + tiles : base + count] = packed[tiles:]
        if base + 2 * tiles < total:
            change = outer(
                jnp.concatenate(packed[:tiles], axis=0),
                jnp.concatenate([packed[t] * inverse_pivot[t] for t in range(tiles)], axis=0),
            )
            for i in range(base + 2 * tiles, total):
                held[i] = jnp.where(in_block, 0.0, held[i]) - change[8 * i : 8 * i + 8, :]


def solve(rows, inverse):
    return lax.dot_general(
        rows, inverse, (((1,), (1,)), ((), ())), preferred_element_type=jnp.float32
    ).astype(jnp.bfloat16)


def gather_kernel(
    diag_ref, panel_ref, trailing_ref,
    solved_ref, solved_cols_ref, slab_ref,
    tile_ref, row_ref, col_ref, inverse_ref, slab_sem,
    tile_send, tile_recv, row_send, row_recv, top_recv, half_send, half_recv, pass_send,
    row_ready, plane_ready,
):
    row, col = lax.axis_index("row"), lax.axis_index("col")
    z, core = row // 2, row % 2
    layers = N // 2
    sibling = (2 * z + 1 - core, col)
    early = z < layers // 2

    source = col // 4
    owner = row == source
    target = 4 * row + col // 4
    size = col_ref.shape[0]
    half = size // 2

    def piece(ref, index, rows):
        return ref.at[pl.ds(pl.multiple_of(index * rows, rows), rows), :]

    def wait_for(ref, sem):
        pltpu.make_async_copy(ref, ref, sem).wait()

    barrier = pltpu.get_barrier_semaphore()

    def greet(device):
        pl.semaphore_signal(barrier, inc=1, device_id=device, device_id_type=MESH)

    for i in range(1, layers):
        greet((2 * lax.rem(z + i, layers), col))
    for i in range(1, N):
        greet((2 * z + 1, lax.rem(col + i, N)))
    greet(sibling)

    own_rows = piece(row_ref, col, PANEL)
    pltpu.make_async_copy(diag_ref, piece(tile_ref, row, 8), tile_recv).start()

    @pl.when(target == col)
    def _():
        pltpu.make_async_copy(panel_ref, own_rows, top_recv).start()

    @pl.when(target != col)
    def _():
        pltpu.make_async_copy(panel_ref, own_rows, row_recv).start()

    def tell(sem):
        pl.semaphore_signal(sem, inc=1, device_id=sibling, device_id_type=MESH)

    def column_is_in():
        @pl.when(core == 0)
        def _():
            pl.semaphore_wait(barrier, N - 1)
            tell(row_ready)

        @pl.when(core == 1)
        def _():
            pl.semaphore_wait(row_ready, 1)

    def plane_is_in():
        @pl.when(core == 1)
        def _():
            pl.semaphore_wait(barrier, 2 * N - 1)
            tell(plane_ready)

        @pl.when(core == 0)
        def _():
            pl.semaphore_wait(plane_ready, 1)

    def send_tile():
        for i in range(1, N):
            pltpu.make_async_remote_copy(
                src_ref=diag_ref, dst_ref=piece(tile_ref, row, 8), send_sem=tile_send, recv_sem=tile_recv,
                device_id=(lax.rem(row + i, N), col), device_id_type=MESH,
            ).start()

    def send_rows(to, recv_sem):
        pltpu.make_async_remote_copy(
            src_ref=panel_ref, dst_ref=own_rows, send_sem=row_send, recv_sem=recv_sem,
            device_id=(row, to), device_id_type=MESH,
        ).start()

    @pl.when(jnp.logical_not(early))
    def _():
        column_is_in()
        send_tile()

    slab_copy = pltpu.make_async_copy(trailing_ref, slab_ref, slab_sem)
    slab_copy.start()
    plane_is_in()

    @pl.when((row < 4) & (target != col))
    def _():
        send_rows(target, top_recv)

    def send_some_rows(first, last):
        for i in range(first, last):
            to = lax.rem(col + i, N)

            @pl.when(to != target)
            def _():
                send_rows(to, row_recv)

    @pl.when(z >= 2)
    def _():
        send_some_rows(1, 16)

    @pl.when((z < 2) & (col >= 4))
    def _():
        send_some_rows(1, 8)

    @pl.when(early)
    def _():
        column_is_in()
        send_tile()

    @pl.when((z < 2) & (col >= 4))
    def _():
        send_some_rows(8, 16)

    @pl.when((z < 2) & (col < 4))
    def _():
        send_some_rows(1, 16)

    own_cols = piece(row_ref, col % 4, size)

    @pl.when(owner)
    def _():
        wait_for(own_cols, top_recv)
        for i in (1, 7, 2, 6, 3 + z, 5, 4 - z):
            for c in range(2):
                pltpu.make_async_remote_copy(
                    src_ref=piece(row_ref, 2 * (col % 4) + c, half), dst_ref=col_ref.at[pl.ds(c * half, half), :],
                    send_sem=half_send, recv_sem=half_recv.at[c],
                    device_id=(2 * lax.rem(z + i, layers) + c, col), device_id_type=MESH,
                ).start()
        for c in range(2):
            here, there = piece(row_ref, 2 * (col % 4) + c, half), col_ref.at[pl.ds(c * half, half), :]
            pltpu.make_async_remote_copy(
                src_ref=here, dst_ref=there, send_sem=half_send, recv_sem=half_recv.at[c],
                device_id=sibling, device_id_type=MESH,
            ).start()
            pltpu.make_async_copy(here, there, half_recv.at[c]).start()

    wait_for(tile_ref, tile_recv)

    my_half = piece(col_ref, core, half)
    passes = z != source // 2

    def between(k):
        if k != PASS_AT:
            return

        @pl.when(passes)
        def _():
            wait_for(my_half, half_recv.at[core])
            pltpu.make_async_remote_copy(
                src_ref=my_half, dst_ref=my_half, send_sem=pass_send, recv_sem=half_recv.at[core],
                device_id=sibling, device_id_type=MESH,
            ).start()

    invert_factor(tile_ref, inverse_ref, between)

    @pl.when(owner)
    def _():
        wait_for(row_ref.at[pl.ds(0, N * PANEL - size), :], row_recv)

    @pl.when(jnp.logical_not(owner))
    def _():
        wait_for(row_ref, row_recv)

    inverse = inverse_ref[...]
    for i in range(row_ref.shape[0] // SOLVED):
        part = pl.ds(i * SOLVED, SOLVED)
        solved_ref[part, :] = solve(row_ref[part, :], inverse)

    def solve_half(c):
        part = pl.ds(pl.multiple_of(c * half, half), half)
        solved_cols_ref[part, :] = solve(col_ref[part, :], inverse)

    @pl.when(passes)
    def _():
        solve_half(core)
        wait_for(piece(col_ref, 1 - core, half), half_recv.at[1 - core])
        solve_half(1 - core)
        wait_for(my_half, pass_send)

    @pl.when(jnp.logical_not(passes))
    def _():
        for c in range(2):
            wait_for(col_ref.at[pl.ds(c * half, half), :], half_recv.at[c])
            solve_half(c)

    slab_copy.wait()
    wait_for(tile_ref.at[pl.ds(0, (N - 1) * 8), :], tile_send)
    wait_for(row_ref.at[pl.ds(0, (N - 1) * PANEL), :], row_send)

    @pl.when(owner)
    def _():
        for _ in range(N * half // row_ref.shape[0]):
            wait_for(row_ref, half_send)


def update_kernel(row_ref, col_ref, slab_ref, solved_ref, updated_ref, out_ref, sems):
    row, col = lax.axis_index("row"), lax.axis_index("col")
    rows, cols = slab_ref.shape
    solved_ref[...] = row_ref[pl.ds(pl.multiple_of(col * PANEL, PANEL), PANEL), :]
    solved_cols = col_ref[...]
    offset = row * rows - col * cols
    below = lax.broadcasted_iota(jnp.int32, (CHUNK, cols), 0) - lax.broadcasted_iota(jnp.int32, (CHUNK, cols), 1)
    copies = []
    for i in range(rows // CHUNK):
        part = pl.ds(i * CHUNK, CHUNK)
        change = lax.dot_general(
            row_ref[part, :], solved_cols, (((1,), (1,)), ((), ())), preferred_element_type=jnp.float32
        )
        lower = below >= -(offset + i * CHUNK)
        old = slab_ref[part, :]
        out_ref[part, :] = jnp.where(lower, old - change, old)
        copy = pltpu.make_async_copy(out_ref.at[part, :], updated_ref.at[part, :], sems.at[i])
        copy.start()
        copies.append(copy)
    for copy in copies:
        copy.wait()


def per_device(diag_tile, panel, trailing):
    rows, cols = trailing.shape
    vmem = pl.BlockSpec(memory_space=pltpu.VMEM)
    hbm = pl.BlockSpec(memory_space=pltpu.HBM)
    dma = pltpu.SemaphoreType.DMA
    gathered = pl.pallas_call(
        gather_kernel,
        out_shape=(
            pltpu.VMEM((rows, PANEL), jnp.bfloat16),
            pltpu.VMEM((cols, PANEL), jnp.bfloat16),
            pltpu.VMEM((rows, cols), jnp.float32),
        ),
        in_specs=[hbm] * 3,
        out_specs=[vmem] * 3,
        scratch_shapes=[
            pltpu.VMEM((PANEL, PANEL), jnp.float32),
            pltpu.VMEM((rows, PANEL), jnp.bfloat16),
            pltpu.VMEM((cols, PANEL), jnp.bfloat16),
            pltpu.VMEM((PANEL, PANEL), jnp.bfloat16),
            dma(()),
            dma(()), dma(()), dma(()), dma(()), dma(()), dma(()), dma((2,)), dma(()),
            pltpu.SemaphoreType.REGULAR, pltpu.SemaphoreType.REGULAR,
        ],
        compiler_params=pltpu.CompilerParams(
            collective_id=0, has_side_effects=True, vmem_limit_bytes=16 << 20
        ),
        name="gather_and_factor",
    )(*[pltpu.with_memory_space_constraint(x, pltpu.HBM) for x in (diag_tile, panel, trailing)])
    return pl.pallas_call(
        update_kernel,
        out_shape=(
            jax.ShapeDtypeStruct((PANEL, PANEL), jnp.bfloat16),
            jax.ShapeDtypeStruct((rows, cols), jnp.float32),
        ),
        in_specs=[vmem] * 3,
        out_specs=[vmem, hbm],
        scratch_shapes=[pltpu.VMEM((rows, cols), jnp.float32), dma((rows // CHUNK,))],
        compiler_params=pltpu.CompilerParams(vmem_limit_bytes=24 << 20),
        name="solve_and_update",
    )(*[pltpu.with_memory_space_constraint(x, pltpu.VMEM) for x in gathered])


def solution(mesh):
    in_specs = (P("row", None), P(("row", "col"), None), P("row", "col"))
    out_specs = (P(("row", "col"), None), P("row", "col"))
    return jax.shard_map(
        per_device, mesh=mesh, in_specs=in_specs, out_specs=out_specs, check_vma=False
    )
```

```python
import functools

import jax
import jax.numpy as jnp
from jax import lax
from jax.experimental import pallas as pl
from jax.experimental.pallas import tpu as pltpu
from jax.sharding import PartitionSpec as P

MESH = pl.DeviceIdType.MESH
N = 16
PANEL = 128
BLOCK = 16
PASS_AT = 7
SOLVED = 512
CHUNK = 256


def spread(tile, sublane):
    return jnp.broadcast_to(tile[sublane : sublane + 1, :], (8, 128))


def split(x):
    high = x.astype(jnp.bfloat16)
    x = x - high.astype(jnp.float32)
    middle = x.astype(jnp.bfloat16)
    return high, middle, (x - middle.astype(jnp.float32)).astype(jnp.bfloat16)


def outer(left, right):
    h, m, l = split(left)
    high, middle, low = split(right)
    return lax.dot_general(
        jnp.concatenate([l, m, h, m, h, h], axis=0),
        jnp.concatenate([high, middle, low, high, middle, high], axis=0),
        (((0,), (0,)), ((), ())),
        preferred_element_type=jnp.float32,
    )


def invert_factor(tile_ref, inverse_ref, between):
    lane = lax.broadcasted_iota(jnp.int32, (8, 128), 1)
    sub = lax.broadcasted_iota(jnp.int32, (8, 128), 0)
    tiles, total = BLOCK // 8, PANEL // 8
    held = [tile_ref[8 * i : 8 * i + 8, :] for i in range(total)]
    for k in range(PANEL // BLOCK):
        between(k)
        first, base = BLOCK * k, tiles * k
        count = min(2 * tiles, total - base)
        rows = held[base : base + count]
        column = [
            [
                jnp.broadcast_to(rows[t][:, first + j : first + j + 1], (8, 128)) if t >= j // 8 else None
                for t in range(count)
            ]
            for j in range(BLOCK)
        ]
        in_block = (lane >= first) & (lane < first + BLOCK)
        packed = [
            jnp.where(in_block, jnp.where(lane - first == sub + 8 * t, 1.0, 0.0) if t < tiles else 0.0, rows[t])
            for t in range(count)
        ]
        inverse_pivot = [None] * tiles
        for j in range(BLOCK):
            tj, sj = divmod(j, 8)
            r = 1.0 / spread(column[j][tj], sj)
            scaled = {t: column[j][t] * r for t in range(tj, count)}
            for m in range(j + 1, BLOCK):
                s = spread(column[j][m // 8], m % 8)
                for t in range(m // 8, count):
                    column[m][t] = column[m][t] - scaled[t] * s
            row = spread(packed[tj], sj)
            for t in range(tj, count):
                if t == tj and sj == 7:
                    continue
                factor = jnp.where(sub > sj, scaled[t], 0.0) if t == tj else scaled[t]
                packed[t] = packed[t] - factor * row
            inverse_pivot[tj] = r if inverse_pivot[tj] is None else jnp.where(sub == sj, r, inverse_pivot[tj])
        inverse = [
            jnp.where(lane < first + BLOCK, packed[t] * jnp.sqrt(inverse_pivot[t]), 0.0) for t in range(tiles)
        ]
        inverse_ref[first : first + BLOCK, :] = jnp.concatenate(inverse, axis=0).astype(jnp.bfloat16)
        held[base + tiles : base + count] = packed[tiles:]
        if base + 2 * tiles < total:
            change = outer(
                jnp.concatenate(packed[:tiles], axis=0),
                jnp.concatenate([packed[t] * inverse_pivot[t] for t in range(tiles)], axis=0),
            )
            for i in range(base + 2 * tiles, total):
                held[i] = jnp.where(in_block, 0.0, held[i]) - change[8 * i : 8 * i + 8, :]


def solve(rows, inverse):
    return lax.dot_general(
        rows, inverse, (((1,), (1,)), ((), ())), preferred_element_type=jnp.float32
    ).astype(jnp.bfloat16)


def gather_kernel(
    diag_ref, panel_ref, trailing_ref,
    solved_ref, solved_cols_ref, slab_ref,
    tile_ref, row_ref, col_ref, inverse_ref, slab_sem,
    tile_send, tile_recv, row_send, row_recv, top_recv, half_send, half_recv, pass_send,
    row_ready, plane_ready,
):
    row, col = lax.axis_index("row"), lax.axis_index("col")
    z, core = row // 2, row % 2
    layers = N // 2
    sibling = (2 * z + 1 - core, col)
    early = z < layers // 2

    source = col // 4
    owner = row == source
    target = 4 * row + col // 4
    size = col_ref.shape[0]
    half = size // 2

    def piece(ref, index, rows):
        return ref.at[pl.ds(pl.multiple_of(index * rows, rows), rows), :]

    def wait_for(ref, sem):
        pltpu.make_async_copy(ref, ref, sem).wait()

    barrier = pltpu.get_barrier_semaphore()

    def greet(device):
        pl.semaphore_signal(barrier, inc=1, device_id=device, device_id_type=MESH)

    for i in range(1, layers):
        greet((2 * lax.rem(z + i, layers), col))
    for i in range(1, N):
        greet((2 * z + 1, lax.rem(col + i, N)))
    greet(sibling)

    own_rows = piece(row_ref, col, PANEL)
    pltpu.make_async_copy(diag_ref, piece(tile_ref, row, 8), tile_recv).start()

    @pl.when(target == col)
    def _():
        pltpu.make_async_copy(panel_ref, own_rows, top_recv).start()

    @pl.when(target != col)
    def _():
        pltpu.make_async_copy(panel_ref, own_rows, row_recv).start()

    def tell(sem):
        pl.semaphore_signal(sem, inc=1, device_id=sibling, device_id_type=MESH)

    def column_is_in():
        @pl.when(core == 0)
        def _():
            pl.semaphore_wait(barrier, N - 1)
            tell(row_ready)

        @pl.when(core == 1)
        def _():
            pl.semaphore_wait(row_ready, 1)

    def plane_is_in():
        @pl.when(core == 1)
        def _():
            pl.semaphore_wait(barrier, 2 * N - 1)
            tell(plane_ready)

        @pl.when(core == 0)
        def _():
            pl.semaphore_wait(plane_ready, 1)

    def send_tile():
        for i in range(1, N):
            pltpu.make_async_remote_copy(
                src_ref=diag_ref, dst_ref=piece(tile_ref, row, 8), send_sem=tile_send, recv_sem=tile_recv,
                device_id=(lax.rem(row + i, N), col), device_id_type=MESH,
            ).start()

    def send_rows(to, recv_sem):
        pltpu.make_async_remote_copy(
            src_ref=panel_ref, dst_ref=own_rows, send_sem=row_send, recv_sem=recv_sem,
            device_id=(row, to), device_id_type=MESH,
        ).start()

    @pl.when(jnp.logical_not(early))
    def _():
        column_is_in()
        send_tile()

    slab_copy = pltpu.make_async_copy(trailing_ref, slab_ref, slab_sem)
    slab_copy.start()
    plane_is_in()

    @pl.when((row < 4) & (target != col))
    def _():
        send_rows(target, top_recv)

    def send_some_rows(first, last):
        for i in range(first, last):
            to = lax.rem(col + i, N)

            @pl.when(to != target)
            def _():
                send_rows(to, row_recv)

    @pl.when(z >= 2)
    def _():
        send_some_rows(1, 16)

    @pl.when((z < 2) & (col >= 4))
    def _():
        send_some_rows(1, 8)

    @pl.when(early)
    def _():
        column_is_in()
        send_tile()

    @pl.when((z < 2) & (col >= 4))
    def _():
        send_some_rows(8, 16)

    @pl.when((z < 2) & (col < 4))
    def _():
        send_some_rows(1, 16)

    own_cols = piece(row_ref, col % 4, size)

    @pl.when(owner)
    def _():
        wait_for(own_cols, top_recv)
        for i in (1, 7, 2, 6, 3 + z, 5, 4 - z):
            for c in range(2):
                pltpu.make_async_remote_copy(
                    src_ref=piece(row_ref, 2 * (col % 4) + c, half), dst_ref=col_ref.at[pl.ds(c * half, half), :],
                    send_sem=half_send, recv_sem=half_recv.at[c],
                    device_id=(2 * lax.rem(z + i, layers) + c, col), device_id_type=MESH,
                ).start()
        for c in range(2):
            here, there = piece(row_ref, 2 * (col % 4) + c, half), col_ref.at[pl.ds(c * half, half), :]
            pltpu.make_async_remote_copy(
                src_ref=here, dst_ref=there, send_sem=half_send, recv_sem=half_recv.at[c],
                device_id=sibling, device_id_type=MESH,
            ).start()
            pltpu.make_async_copy(here, there, half_recv.at[c]).start()

    wait_for(tile_ref, tile_recv)

    my_half = piece(col_ref, core, half)
    passes = z != source // 2

    def between(k):
        if k != PASS_AT:
            return

        @pl.when(passes)
        def _():
            wait_for(my_half, half_recv.at[core])
            pltpu.make_async_remote_copy(
                src_ref=my_half, dst_ref=my_half, send_sem=pass_send, recv_sem=half_recv.at[core],
                device_id=sibling, device_id_type=MESH,
            ).start()

    invert_factor(tile_ref, inverse_ref, between)

    @pl.when(owner)
    def _():
        wait_for(row_ref.at[pl.ds(0, N * PANEL - size), :], row_recv)

    @pl.when(jnp.logical_not(owner))
    def _():
        wait_for(row_ref, row_recv)

    inverse = inverse_ref[...]
    for i in range(row_ref.shape[0] // SOLVED):
        part = pl.ds(i * SOLVED, SOLVED)
        solved_ref[part, :] = solve(row_ref[part, :], inverse)

    def solve_half(c):
        part = pl.ds(pl.multiple_of(c * half, half), half)
        solved_cols_ref[part, :] = solve(col_ref[part, :], inverse)

    @pl.when(passes)
    def _():
        solve_half(core)
        wait_for(piece(col_ref, 1 - core, half), half_recv.at[1 - core])
        solve_half(1 - core)
        wait_for(my_half, pass_send)

    @pl.when(jnp.logical_not(passes))
    def _():
        for c in range(2):
            wait_for(col_ref.at[pl.ds(c * half, half), :], half_recv.at[c])
            solve_half(c)

    slab_copy.wait()
    wait_for(tile_ref.at[pl.ds(0, (N - 1) * 8), :], tile_send)
    wait_for(row_ref.at[pl.ds(0, (N - 1) * PANEL), :], row_send)

    @pl.when(owner)
    def _():
        for _ in range(N * half // row_ref.shape[0]):
            wait_for(row_ref, half_send)


def update_kernel(row_ref, col_ref, slab_ref, solved_ref, updated_ref, out_ref, sems):
    row, col = lax.axis_index("row"), lax.axis_index("col")
    rows, cols = slab_ref.shape
    solved_ref[...] = row_ref[pl.ds(pl.multiple_of(col * PANEL, PANEL), PANEL), :]
    solved_cols = col_ref[...]
    offset = row * rows - col * cols
    below = lax.broadcasted_iota(jnp.int32, (CHUNK, cols), 0) - lax.broadcasted_iota(jnp.int32, (CHUNK, cols), 1)
    copies = []
    starts = [0] + [CHUNK // 2 + i * CHUNK for i in range(rows // CHUNK)] + [rows]
    for i, (start, end) in enumerate(zip(starts, starts[1:])):
        part = pl.ds(start, end - start)
        change = lax.dot_general(
            row_ref[part, :], solved_cols, (((1,), (1,)), ((), ())), preferred_element_type=jnp.float32
        )
        lower = below[: end - start] >= -(offset + start)
        old = slab_ref[part, :]
        out_ref[part, :] = jnp.where(lower, old - change, old)
        copy = pltpu.make_async_copy(out_ref.at[part, :], updated_ref.at[part, :], sems.at[i])
        copy.start()
        copies.append(copy)
    for copy in copies:
        copy.wait()


def per_device(diag_tile, panel, trailing):
    rows, cols = trailing.shape
    vmem = pl.BlockSpec(memory_space=pltpu.VMEM)
    hbm = pl.BlockSpec(memory_space=pltpu.HBM)
    dma = pltpu.SemaphoreType.DMA
    gathered = pl.pallas_call(
        gather_kernel,
        out_shape=(
            pltpu.VMEM((rows, PANEL), jnp.bfloat16),
            pltpu.VMEM((cols, PANEL), jnp.bfloat16),
            pltpu.VMEM((rows, cols), jnp.float32),
        ),
        in_specs=[hbm] * 3,
        out_specs=[vmem] * 3,
        scratch_shapes=[
            pltpu.VMEM((PANEL, PANEL), jnp.float32),
            pltpu.VMEM((rows, PANEL), jnp.bfloat16),
            pltpu.VMEM((cols, PANEL), jnp.bfloat16),
            pltpu.VMEM((PANEL, PANEL), jnp.bfloat16),
            dma(()),
            dma(()), dma(()), dma(()), dma(()), dma(()), dma(()), dma((2,)), dma(()),
            pltpu.SemaphoreType.REGULAR, pltpu.SemaphoreType.REGULAR,
        ],
        compiler_params=pltpu.CompilerParams(
            collective_id=0, has_side_effects=True, vmem_limit_bytes=16 << 20
        ),
        name="gather_and_factor",
    )(*[pltpu.with_memory_space_constraint(x, pltpu.HBM) for x in (diag_tile, panel, trailing)])
    return pl.pallas_call(
        update_kernel,
        out_shape=(
            jax.ShapeDtypeStruct((PANEL, PANEL), jnp.bfloat16),
            jax.ShapeDtypeStruct((rows, cols), jnp.float32),
        ),
        in_specs=[vmem] * 3,
        out_specs=[vmem, hbm],
        scratch_shapes=[pltpu.VMEM((rows, cols), jnp.float32), dma((rows // CHUNK + 1,))],
        compiler_params=pltpu.CompilerParams(vmem_limit_bytes=24 << 20),
        name="solve_and_update",
    )(*[pltpu.with_memory_space_constraint(x, pltpu.VMEM) for x in gathered])


def solution(mesh):
    in_specs = (P("row", None), P(("row", "col"), None), P("row", "col"))
    out_specs = (P(("row", "col"), None), P("row", "col"))
    return jax.shard_map(
        per_device, mesh=mesh, in_specs=in_specs, out_specs=out_specs, check_vma=False
    )
```
